256 devices in a mesh: wide: 64 (over z, y, core), narrow: 4 (over x).
Axes of the slice: x: 4, y: 4, z: 8, core: 2. Of those that a mesh axis runs over, the one named last changes fastest.
Arguments:
- xblk: bfloat16 [3, 576, 9, 16384], P(None, 'narrow', None, 'wide')
- link: int32 [256], replicated, may hold values from 0 to 1, as said below
- order: int32 [16384], P('wide'), may hold values from 0 to 255, as said below
Outputs:
- relaid: bfloat16 [9, 5, 576, 16384], P(None, None, 'narrow', 'wide')
The draws below stay inside these ranges and needn't reach their ends.
Inputs may be any that keep to these rules, and one draw needn't show every extreme that they name: `order`: each aligned run of 256 entries is a permutation of 0 to 255. link[r] is 0 or 1 for every r.
All inputs are finite; a program needn't handle non-finite values.
Results may differ from the reference program's by a relative error of at most 0.001.
Values may be sent and summed in bfloat16 or wider, within the bound.
No kernel may reach another device: no remote copies, remote signals or barrier semaphores. Data moves between devices by JAX's collectives and lax.ppermute only.
A program may use at most 192 MiB of HBM per device.

```python
import math
import jax
import jax.numpy as jnp
from jax import lax

ORBITALS = 9
BLOCK_ATOMS = 64
BLOCK = 576
RB = 4
NR = 256
ATOMS_DEV = 256
NATOMS = 16384
N_WIDE = 64


def draw_xblk(key, part):
    key = jax.random.fold_in(key, 11)
    first_key, second_key, level_key, shift_key, scale_key = jax.random.split(key, 5)
    spread = 1.0 / math.sqrt(2.5 * BLOCK)
    upper = jax.random.normal(first_key, (NR, BLOCK, BLOCK), jnp.float32) * spread
    base = jax.random.normal(second_key, (NR, BLOCK, BLOCK), jnp.float32) * (spread / math.sqrt(2.0))
    level = jax.random.uniform(level_key, (), jnp.float32, 0.6, 1.4)
    shifts = level + jax.random.uniform(shift_key, (NR,), jnp.float32, -0.35, 0.35)
    scales = jax.random.uniform(scale_key, (NR,), jnp.float32, 0.5, 1.5)
    upper = upper * scales[:, None, None]
    diagonal = base + jnp.swapaxes(base, 1, 2) + shifts[:, None, None] * jnp.eye(BLOCK, dtype=jnp.float32)
    lower = jnp.swapaxes(jnp.roll(upper, 1, axis=0), 1, 2)
    stored = jnp.stack([lower, diagonal, upper], axis=1)
    shaped = stored.reshape(NR, 3, BLOCK_ATOMS, ORBITALS, BLOCK)
    laid = jnp.transpose(shaped, (1, 4, 3, 0, 2)).reshape(3, BLOCK, ORBITALS, NATOMS)
    return laid.astype(jnp.bfloat16)


def draw_link(key, part):
    key = jax.random.fold_in(key, 37)
    coins = jax.random.randint(key, (NR,), 0, 4)
    random_links = jnp.where(coins < 3, 1, 0).astype(jnp.int32)
    positions = jnp.arange(NR, dtype=jnp.int32)
    boundary = positions % RB == RB - 1
    return jnp.where(boundary, 1, random_links).astype(jnp.int32)


def draw_order(key, part):
    key = jax.random.fold_in(key, 23)
    keys = jax.random.split(key, N_WIDE)
    shuffled = jax.vmap(lambda single: jax.random.permutation(single, ATOMS_DEV))(keys)
    return shuffled.reshape(-1).astype(jnp.int32)


def setup_inputs(seed: int = 0) -> dict:
    splits = jax.random.split(jax.random.key(seed), 4)
    xblk = draw_xblk(jax.random.fold_in(splits[3], 71), 0)
    link = draw_link(jax.random.fold_in(splits[3], 71), 0)
    order = draw_order(jax.random.fold_in(splits[3], 71), 0)
    return dict(xblk=xblk, link=link, order=order)


def masked_blocks(xblk, link):
    total_rows = link.shape[0]
    shaped = xblk.reshape(3, BLOCK, ORBITALS, total_rows, BLOCK_ATOMS)
    stored = jnp.transpose(shaped, (3, 0, 4, 2, 1)).reshape(total_rows, 3, BLOCK, BLOCK)
    present = link.astype(jnp.bfloat16)
    previous = jnp.roll(present, 1)
    factors = jnp.stack([previous, jnp.ones_like(present), present], axis=1)
    return stored * factors[:, :, None, None]


def reference(xblk, link, order):
    blocks = masked_blocks(xblk, link)
    total_rows = blocks.shape[0]

    def row_product(row_id):
        pieces = []
        for target in range(-2, 3):
            summed = jnp.zeros((BLOCK, BLOCK), jnp.float32)
            for offset in range(-1, 2):
                partner = target - offset
                if abs(partner) <= 1:
                    left_block = blocks[row_id, offset + 1]
                    right_block = blocks[(row_id + offset) % total_rows, partner + 1]
                    summed = summed + jnp.dot(left_block, right_block, preferred_element_type=jnp.float32)
            pieces.append(summed)
        return jnp.stack(pieces)

    product = lax.map(row_product, jnp.arange(total_rows, dtype=jnp.int32))
    trace_x = jnp.sum(jnp.diagonal(blocks[:, 1], axis1=1, axis2=2).astype(jnp.float32))
    trace_sq = jnp.sum(jnp.diagonal(product[:, 2], axis1=1, axis2=2))
    weight = jax.nn.sigmoid(4.0 * (trace_x - trace_sq) / (total_rows * BLOCK) + 5.0)
    edge = jnp.zeros_like(product[:, :1])
    padded = jnp.concatenate([edge, blocks.astype(jnp.float32), edge], axis=1)
    fresh = (product + 2.0 * weight * (padded - product)).astype(jnp.bfloat16)
    atom_count = BLOCK // ORBITALS
    shaped = fresh.reshape(total_rows, 5, atom_count, ORBITALS, BLOCK)
    atoms = jnp.transpose(shaped, (0, 2, 3, 1, 4)).reshape(total_rows * atom_count, ORBITALS, 5, BLOCK)
    group_size = ATOMS_DEV // N_WIDE
    bases = (jnp.arange(N_WIDE, dtype=jnp.int32) * ATOMS_DEV)[:, None, None]
    source = order.reshape(N_WIDE, N_WIDE, group_size) + bases
    source = jnp.transpose(source, (1, 0, 2)).reshape(-1)
    taken = jnp.take(atoms, source, axis=0)
    return jnp.transpose(taken, (1, 2, 3, 0))
```

```python
import functools
import jax
import jax.numpy as jnp
import numpy as np
from jax import lax
from jax.experimental import pallas as pl
from jax.experimental.pallas import tpu as pltpu
from jax.sharding import PartitionSpec as P

ORB = 9
ATOMS = 64
BLOCK = 576
PANEL = 144
LANES = 640
ROWS = 4
NARROW = 4
WIDE = 64
SLABS = 5
MAIN = 512
CHUNK = 1664
QUARTERS = ((0, 192), (192, 384), (384, 560), (560, 720))
F32 = jnp.float32
BF16 = jnp.bfloat16
VMEM_LIMIT = 58 * 1024 * 1024

VM = pl.BlockSpec(memory_space=pltpu.VMEM)
SM = pl.BlockSpec(memory_space=pltpu.SMEM)


def params():
    return pltpu.CompilerParams(vmem_limit_bytes=VMEM_LIMIT)


def one_hot(rows, cols, wanted):
    lanes = lax.broadcasted_iota(jnp.int32, (rows, cols), 1)
    return jnp.where(lanes == wanted, 1.0, 0.0).astype(BF16)


def lane_mask(link, first, shift):
    lanes = lax.broadcasted_iota(jnp.int32, (1, ROWS * ATOMS), 1) // ATOMS
    total = link.shape[0]
    mask = jnp.zeros((1, ROWS * ATOMS), F32)
    for r in range(ROWS):
        value = link[lax.rem(first + (r + shift + total), total)].astype(F32)
        mask = jnp.where(lanes == r, value, mask)
    return mask


def prep_kernel(link, pos, x, ga, gb, a_first, a_mid, a_last):
    first = pos[0] * ROWS
    masks = (
        lane_mask(link, first, -1).astype(BF16),
        None,
        lane_mask(link, first, 0).astype(BF16),
    )
    i = lax.broadcasted_iota(jnp.int32, (PANEL, PANEL), 0)
    c = lax.broadcasted_iota(jnp.int32, (PANEL, PANEL), 1)
    reorder = jnp.where(c == (i % 16) * ORB + i // 16, 1.0, 0.0).astype(BF16)
    zeros = jnp.zeros((PANEL, ATOMS), BF16)

    def row(tiles, r):
        parts = [t[:, r * ATOMS : (r + 1) * ATOMS] for t in tiles] + [zeros]
        return jnp.concatenate(parts, axis=1)

    for j in range(3):
        tiles = [x[j, o] for o in range(ORB)]
        if masks[j] is not None:
            tiles = [t * masks[j] for t in tiles]
        for r in range(ROWS):
            value = row(tiles, r)
            if r == 0:
                a_first[j] = value
            elif r == ROWS - 1:
                a_last[j] = value
            else:
                a_mid[r - 1, j] = value
            turned = None
            if j < 2 or r == ROWS - 1:
                turned = jnp.dot(reorder, value, preferred_element_type=F32).astype(BF16)
            if j == 0:
                ga[r] = turned
            elif j == 1:
                gb[r] = turned
            elif r == ROWS - 1:
                ga[ROWS] = turned


def trace_kernel(link, pos, x, out):
    first = pos[0] * ROWS
    narrow = pos[1]
    masks = (lane_mask(link, first, -1), None, lane_mask(link, first, 0))
    squares = jnp.zeros((PANEL, ROWS * ATOMS), F32)
    for j in range(3):
        total = jnp.zeros((PANEL, ROWS * ATOMS), F32)
        for o in range(ORB):
            t = x[j, o].astype(F32)
            total = total + t * t
        if masks[j] is not None:
            total = total * masks[j]
        squares = squares + total
    rows = lax.broadcasted_iota(jnp.int32, (PANEL, ROWS * ATOMS), 0) + narrow * PANEL
    lanes = lax.broadcasted_iota(jnp.int32, (PANEL, ROWS * ATOMS), 1) % ATOMS
    diagonal = jnp.zeros((PANEL, ROWS * ATOMS), F32)
    for o in range(ORB):
        diagonal = diagonal + jnp.where(rows == lanes * ORB + o, x[1, o].astype(F32), 0.0)
    sq = jnp.sum(squares, axis=0, keepdims=True)
    tx = jnp.sum(diagonal, axis=0, keepdims=True)
    sq = jnp.sum(sq, axis=1, keepdims=True)
    tx = jnp.sum(tx, axis=1, keepdims=True)
    lane = lax.broadcasted_iota(jnp.int32, (1, 128), 1)
    out[...] = jnp.where(lane == 0, tx, jnp.where(lane == 1, sq, 0.0))


def deal_kernel(want_quad, want_last, quad, last):
    step = 128
    for k in range(0, 1024, step):
        quad[k : k + step, :] = one_hot(step, 1024, want_quad[k : k + step, :])
        last[k : k + step, :] = one_hot(step, 1024, want_last[k : k + step, :])


def nt(a, b):
    return lax.dot_general(a, b, (((1,), (1,)), ((), ())), preferred_element_type=F32)


def tn(a, b):
    return lax.dot_general(a, b, (((0,), (0,)), ((), ())), preferred_element_type=F32)


def product_kernel(
    weight, pos,
    ga0, ga1, ga2, ga3, gb0, gb1, gb2, gb3,
    a_prev, a_first, a_mid, a_last, a_next, quad, last,
    out, full, acc, fresh, fresh_last,
):
    narrow = pos[1]
    twice = 2.0 * weight[0]
    for shift, (a, b) in enumerate(((ga0, gb0), (ga1, gb1), (ga2, gb2), (ga3, gb3))):
        owner = lax.rem(narrow + shift, NARROW)
        for p in range(9):
            src = a[p] if p < 5 else b[p - 5]
            full[p, :, pl.ds(owner, 1)] = src.reshape(ORB, 1, 16, LANES)
    lefts = [
        lambda j: a_prev[j],
        lambda j: a_first[j],
        lambda j: a_mid[0, j],
        lambda j: a_mid[1, j],
        lambda j: a_last[j],
        lambda j: a_next[j],
    ]

    def left(r):
        return jnp.concatenate([lefts[r + 1](j)[:, :BLOCK] for j in range(3)], axis=0)

    def block(p):
        return full[p].reshape(BLOCK, LANES)

    fresh_last[...] = jnp.zeros_like(fresh_last)
    for r in range(ROWS):
        acc[...] = jnp.zeros_like(acc)
        for d in range(-1, 2):
            stack = left(r + d)
            if d == -1:
                value = jnp.dot(stack, block(r), preferred_element_type=F32)
            elif d == 0:
                value = jnp.dot(stack, block(5 + r), preferred_element_type=F32)
            elif r < ROWS - 1:
                value = nt(stack, block(r + 1)[:, :BLOCK])
            else:
                value = jnp.dot(stack, block(4), preferred_element_type=F32)
            for j in range(3):
                e = d + j - 1
                piece = value[j * PANEL : (j + 1) * PANEL]
                if piece.shape[1] == BLOCK:
                    acc[e + 2, :, :BLOCK] += piece
                else:
                    acc[e + 2] += piece
        for s in range(SLABS):
            prod = acc[s]
            if 1 <= s <= 3:
                start = lefts[r + 1](s - 1).astype(F32)
                value = prod + twice * (start - prod)
            else:
                value = prod + twice * (0.0 - prod)
            fresh[s, :, r * MAIN : (r + 1) * MAIN] = value[:, :MAIN].astype(BF16)
            tail = value[:, MAIN:].astype(BF16)
            for q, (low, high) in enumerate(QUARTERS):
                begin, end = max(low, s * PANEL), min(high, (s + 1) * PANEL)
                if begin < end:
                    lane = q * 256 + r * ATOMS
                    fresh_last[begin - low : end - low, lane : lane + ATOMS] = tail[
                        begin - s * PANEL : end - s * PANEL, :ATOMS
                    ]
    rems = []
    for g in range(2):
        lanes = [slice(r * MAIN + g * 256, r * MAIN + g * 256 + 256) for r in range(ROWS)]
        main = jnp.concatenate([fresh[:, :128, l].reshape(SLABS * 128, 256) for l in lanes], axis=1)
        rem = jnp.concatenate([fresh[:, 128:, l].reshape(SLABS * 16, 256) for l in lanes], axis=1)
        out[:, g * 640 : (g + 1) * 640] = nt(quad[...], main).astype(BF16)
        rems.append(nt(quad[...], rem))
    rems.append(nt(last[...], fresh_last[...]))
    rems.append(jnp.zeros((1024, 32), F32))
    out[:, 1280:] = jnp.concatenate(rems, axis=1).astype(BF16)


def unpack_kernel(z, spread, out):
    for g in range(2):
        main = tn(z[:, g * 640 : (g + 1) * 640], spread[...]).astype(BF16)
        for q in range(4):
            for s in range(SLABS):
                out[g * 4 + q, s * PANEL : s * PANEL + 128, :] = main[
                    s * 128 : (s + 1) * 128, q * 256 : (q + 1) * 256
                ]
    rest = tn(z[:, 1280:], spread[...]).astype(BF16)
    for g in range(2):
        for q in range(4):
            for s in range(SLABS):
                out[g * 4 + q, s * PANEL + 128 : (s + 1) * PANEL, :] = rest[
                    g * 80 + s * 16 : g * 80 + s * 16 + 16, q * 256 : (q + 1) * 256
                ]
    for q, (low, high) in enumerate(QUARTERS):
        out[8, low:high, :] = rest[160 : 160 + high - low, q * 256 : (q + 1) * 256]


def spread_matrix():
    w, q, j = np.meshgrid(np.arange(64), np.arange(4), np.arange(4), indexing="ij")
    table = np.zeros((1024, 1024), np.float32)
    table[np.arange(1024), (q * 256 + w * 4 + j).reshape(-1)] = 1.0
    return table


def shift_perm(count, step):
    return [(i, (i - step) % count) for i in range(count)]


def total_sum(value):
    for axis, count, strides in (("narrow", 4, (1,)), ("wide", 64, (1, 4, 16))):
        for stride in strides:
            others = []
            for m in (1, 2, 3):
                perm = []
                for i in range(count):
                    digit = (i // stride) % 4
                    perm.append((i, i + (((digit + m) % 4) - digit) * stride))
                others.append(lax.ppermute(value, axis, perm))
            value = value + others[0] + others[1] + others[2]
    return value


def shards(xblk, link, order):
    wide_pos = lax.axis_index("wide")
    narrow_pos = lax.axis_index("narrow")
    pos = jnp.stack([wide_pos, narrow_pos]).astype(jnp.int32)
    x = jnp.transpose(xblk, (0, 2, 1, 3))
    sds = jax.ShapeDtypeStruct
    ga, gb, a_first, a_mid, a_last = pl.pallas_call(
        prep_kernel,
        out_shape=[
            sds((5, PANEL, LANES), BF16),
            sds((4, PANEL, LANES), BF16),
            sds((3, PANEL, LANES), BF16),
            sds((2, 3, PANEL, LANES), BF16),
            sds((3, PANEL, LANES), BF16),
        ],
        in_specs=[SM, SM, VM],
        out_specs=[VM] * 5,
        compiler_params=params(),
        name="prep",
    )(link, pos, x)
    gas, gbs = [ga], [gb]
    for step in (1, 2, 3):
        gas.append(lax.ppermute(ga, "narrow", shift_perm(NARROW, step)))
    a_prev = lax.ppermute(a_last, "wide", shift_perm(WIDE, -1))
    a_next = lax.ppermute(a_first, "wide", shift_perm(WIDE, 1))
    for step in (1, 2, 3):
        gbs.append(lax.ppermute(gb, "narrow", shift_perm(NARROW, step)))
    traces = pl.pallas_call(
        trace_kernel,
        out_shape=sds((1, 128), F32),
        in_specs=[SM, SM, VM],
        out_specs=VM,
        compiler_params=params(),
        name="traces",
    )(link, pos, x)
    sums = total_sum(traces)
    weight = jax.nn.sigmoid(4.0 * (sums[0, 0] - sums[0, 1]) / (link.shape[0] * BLOCK) + 5.0)
    wanted = jnp.broadcast_to(order.reshape(64, 1, 4), (64, 4, 4))
    quarter = jnp.arange(4, dtype=jnp.int32).reshape(1, 4, 1)
    want_quad = ((wanted // ATOMS) * 256 + quarter * ATOMS + wanted % ATOMS).reshape(1024, 1)
    want_last = (quarter * 256 + wanted).reshape(1024, 1)
    quad, last = pl.pallas_call(
        deal_kernel,
        out_shape=[sds((1024, 1024), BF16)] * 2,
        in_specs=[VM, VM],
        out_specs=[VM] * 2,
        compiler_params=params(),
        name="deal",
    )(want_quad, want_last)
    packed = pl.pallas_call(
        product_kernel,
        out_shape=sds((1024, CHUNK), BF16),
        in_specs=[SM, SM] + [VM] * 15,
        out_specs=VM,
        scratch_shapes=[
            pltpu.VMEM((9, ORB, NARROW, 16, LANES), BF16),
            pltpu.VMEM((SLABS, PANEL, LANES), F32),
            pltpu.VMEM((SLABS, PANEL, ROWS * MAIN), BF16),
            pltpu.VMEM((192, 1024), BF16),
        ],
        compiler_params=params(),
        name="product",
    )(weight.reshape(1), pos, *gas, *gbs, a_prev, a_first, a_mid, a_last, a_next, quad, last)
    received = lax.all_to_all(
        packed.reshape(WIDE, 16, CHUNK), "wide", split_axis=0, concat_axis=0, tiled=True
    )
    spread = jnp.asarray(spread_matrix(), BF16)
    out = pl.pallas_call(
        unpack_kernel,
        out_shape=sds((ORB, SLABS * PANEL, 256), BF16),
        in_specs=[VM, VM],
        out_specs=VM,
        compiler_params=params(),
        name="unpack",
    )(received.reshape(1024, CHUNK), spread)
    return out.reshape(ORB, SLABS, PANEL, 256)


def solution(mesh):
    return jax.shard_map(
        shards,
        mesh=mesh,
        in_specs=(P(None, "narrow", None, "wide"), P(), P("wide")),
        out_specs=P(None, None, "narrow", "wide"),
        check_vma=False,
    )
```

```python
import jax
import jax.numpy as jnp
import numpy as np
from jax import lax
from jax.experimental import pallas as pl
from jax.experimental.pallas import tpu as pltpu
from jax.sharding import PartitionSpec as P

ORB = 9
ATOMS = 64
BLOCK = 576
PANEL = 144
LANES = 640
ROWS = 4
NARROW = 4
WIDE = 64
MAIN = 512
OUTER_CHUNK = 640
INNER_CHUNK = 1024
INNER_QUARTERS = ((0, 112), (112, 224), (224, 336), (336, 432))
F32 = jnp.float32
BF16 = jnp.bfloat16
OUTER_FLOPS = 30 * 10**9
INNER_FLOPS = 70 * 10**9
VMEM_LIMIT = 56 * 1024 * 1024

VM = pl.BlockSpec(memory_space=pltpu.VMEM)
SM = pl.BlockSpec(memory_space=pltpu.SMEM)
ANY = pl.BlockSpec(memory_space=pl.ANY)
sds = jax.ShapeDtypeStruct


def params():
    return pltpu.CompilerParams(vmem_limit_bytes=VMEM_LIMIT)


def lane_mask(link, first, shift):
    lanes = lax.broadcasted_iota(jnp.int32, (1, ROWS * ATOMS), 1) // ATOMS
    total = link.shape[0]
    mask = jnp.zeros((1, ROWS * ATOMS), F32)
    for r in range(ROWS):
        value = link[lax.rem(first + (r + shift + total), total)].astype(F32)
        mask = jnp.where(lanes == r, value, mask)
    return mask


def reorder_matrix():
    i = lax.broadcasted_iota(jnp.int32, (PANEL, PANEL), 0)
    c = lax.broadcasted_iota(jnp.int32, (PANEL, PANEL), 1)
    return jnp.where(c == (i % 16) * ORB + i // 16, 1.0, 0.0).astype(BF16)


def packed_row(tiles, r, pad):
    parts = [t[:, r * ATOMS : (r + 1) * ATOMS] for t in tiles]
    if pad:
        parts.append(jnp.zeros((PANEL, ATOMS), BF16))
    return jnp.concatenate(parts, axis=1)


def put_panel(out, count, p, value):
    out[:, p * MAIN : (p + 1) * MAIN] = value[:, :MAIN]
    tail = count * MAIN + p * ATOMS
    out[:, tail : tail + ATOMS] = value[:, MAIN:BLOCK]


def prep_kernel(link, x, traces, ga, gb, a_first, a_mid, a_last):
    del traces
    first = lax.axis_index("wide") * ROWS
    masks = (
        lane_mask(link, first, -1).astype(BF16),
        None,
        lane_mask(link, first, 0).astype(BF16),
    )
    reorder = reorder_matrix()
    for j in range(3):
        tiles = [x[j, o] for o in range(ORB)]
        if masks[j] is not None:
            tiles = [t * masks[j] for t in tiles]
        for r in range(ROWS):
            value = packed_row(tiles, r, True)
            if r == 0:
                a_first[j] = value
            elif r == ROWS - 1:
                a_last[j] = value
            else:
                a_mid[r - 1, j] = value
            if j == 2 and r < ROWS - 1:
                continue
            turned = jnp.dot(reorder, value, preferred_element_type=F32).astype(BF16)
            if j == 1:
                put_panel(gb, ROWS, r, turned)
            else:
                put_panel(ga, ROWS + 1, r if j == 0 else ROWS, turned)
    ga[:, (ROWS + 1) * BLOCK :] = jnp.zeros((PANEL, ATOMS), BF16)


def trace_kernel(link, x, out):
    first = lax.axis_index("wide") * ROWS
    narrow = lax.axis_index("narrow")
    masks = (lane_mask(link, first, -1), None, lane_mask(link, first, 0))
    squares = jnp.zeros((PANEL, ROWS * ATOMS), F32)
    for j in range(3):
        total = jnp.zeros((PANEL, ROWS * ATOMS), F32)
        for o in range(ORB):
            t = x[j, o].astype(F32)
            total = total + t * t
        if masks[j] is not None:
            total = total * masks[j]
        squares = squares + total
    rows = lax.broadcasted_iota(jnp.int32, (PANEL, ROWS * ATOMS), 0) + narrow * PANEL
    lanes = lax.broadcasted_iota(jnp.int32, (PANEL, ROWS * ATOMS), 1) % ATOMS
    diagonal = jnp.zeros((PANEL, ROWS * ATOMS), F32)
    for o in range(ORB):
        diagonal = diagonal + jnp.where(rows == lanes * ORB + o, x[1, o].astype(F32), 0.0)
    sq = jnp.sum(squares, axis=0, keepdims=True)
    tx = jnp.sum(diagonal, axis=0, keepdims=True)
    sq = jnp.sum(sq, axis=1, keepdims=True)
    tx = jnp.sum(tx, axis=1, keepdims=True)
    lane = lax.broadcasted_iota(jnp.int32, (1, 128), 1)
    out[...] = jnp.where(lane == 0, tx, jnp.where(lane == 1, sq, 0.0))


def deal_kernel(wanted, quad):
    step = 128
    for k in range(0, 1024, step):
        lanes = lax.broadcasted_iota(jnp.int32, (step, 1024), 1)
        quad[k : k + step, :] = jnp.where(lanes == wanted[k : k + step, :], 1.0, 0.0).astype(BF16)


def nt(a, b):
    return lax.dot_general(a, b, (((1,), (1,)), ((), ())), preferred_element_type=F32)


def tn(a, b):
    return lax.dot_general(a, b, (((0,), (0,)), ((), ())), preferred_element_type=F32)


def twice_weight(sums, rows_total):
    total = jnp.sum(sums[...], axis=0)
    tx = total[:, 0:1]
    sq = total[:, 1:2]
    return 2.0 * jax.nn.sigmoid(4.0 * (tx - sq) / (rows_total * BLOCK) + 5.0)


def assemble(full, base, count, sources):
    narrow = lax.axis_index("narrow")
    for shift, src in enumerate(sources):
        owner = lax.rem(narrow + shift, NARROW)
        for p in range(count):
            value = src[:, p * MAIN : (p + 1) * MAIN]
            full[base + p, :, pl.ds(owner, 1), :, :MAIN] = value.reshape(
                ORB, 1, 16, MAIN
            )
            tail = count * MAIN + p * ATOMS
            value = src[:, tail : tail + ATOMS]
            full[base + p, :, pl.ds(owner, 1), :, MAIN:BLOCK] = value.reshape(
                ORB, 1, 16, ATOMS
            )


def deal(quad, fresh, group, slabs):
    lanes = [slice(r * MAIN + group * 256, r * MAIN + group * 256 + 256) for r in range(ROWS)]
    main = jnp.concatenate([fresh[:, :128, l].reshape(slabs * 128, 256) for l in lanes], axis=1)
    rem = jnp.concatenate([fresh[:, 128:, l].reshape(slabs * 16, 256) for l in lanes], axis=1)
    return nt(quad[...], main), nt(quad[...], rem)


def outer_kernel(
    rows_total, sums, ga0, ga1, ga2, ga3, a_prev, a_first, a_mid, a_last, a_next, quad,
    out, left_over, full, fresh, last,
):
    gas = (ga0, ga1, ga2, ga3)
    twice = twice_weight(sums, rows_total)
    assemble(full, 0, ROWS + 1, gas)
    lefts = [a_prev, a_first, a_mid.at[0], a_mid.at[1], a_last, a_next]
    left_over[...] = jnp.zeros_like(left_over)
    for r in range(ROWS):
        for s in range(2):
            if s == 0:
                b = full[r].reshape(BLOCK, LANES)
                prod = jnp.dot(lefts[r][0][:, :BLOCK], b, preferred_element_type=F32)
            elif r < ROWS - 1:
                b = full[r + 1].reshape(BLOCK, LANES)[:, :BLOCK]
                prod = nt(lefts[r + 2][2][:, :BLOCK], b)
            else:
                b = full[ROWS].reshape(BLOCK, LANES)
                prod = jnp.dot(lefts[r + 2][2][:, :BLOCK], b, preferred_element_type=F32)
            value = prod + twice * (0.0 - prod)
            fresh[s, :, r * MAIN : (r + 1) * MAIN] = value[:, :MAIN].astype(BF16)
            tail = value[:, MAIN:BLOCK].astype(BF16)
            for half in range(2):
                lane = r * 256 + (2 * s + half) * ATOMS
                last[:, lane : lane + ATOMS] = tail[half * 64 : half * 64 + 64]
            lane = r * 256 + s * ATOMS
            left_over[:, lane : lane + ATOMS] = tail[128:]
    rems = []
    for g in range(2):
        main, rem = deal(quad, fresh, g, 2)
        out[:, g * 256 : (g + 1) * 256] = main.astype(BF16)
        rems.append(rem)
    rems.append(nt(quad[...], last[...]))
    out[:, 512:] = jnp.concatenate(rems, axis=1).astype(BF16)


def inner_kernel(
    rows_total, sums, ga0, ga1, ga2, ga3, gb0, gb1, gb2, gb3,
    a_prev, a_first, a_mid, a_last, a_next, quad, left_over,
    out, full, acc, fresh, last,
):
    gas = (ga0, ga1, ga2, ga3)
    gbs = (gb0, gb1, gb2, gb3)
    twice = twice_weight(sums, rows_total)
    assemble(full, 0, ROWS + 1, gas)
    assemble(full, ROWS + 1, ROWS, gbs)
    lefts = [a_prev, a_first, a_mid.at[0], a_mid.at[1], a_last, a_next]

    def left(r, low, high):
        return jnp.concatenate([lefts[r + 1][j][:, :BLOCK] for j in range(low, high)], axis=0)

    last[112:, :] = left_over[...]
    last[96:112, :] = jnp.zeros((16, 1024), BF16)
    for r in range(ROWS):
        value = jnp.dot(
            left(r, 0, 3), full[ROWS + 1 + r].reshape(BLOCK, LANES), preferred_element_type=F32
        )
        for s in range(3):
            acc[s] = value[s * PANEL : (s + 1) * PANEL]
        value = jnp.dot(
            left(r - 1, 1, 3), full[r].reshape(BLOCK, LANES), preferred_element_type=F32
        )
        for s in range(2):
            acc[s] += value[s * PANEL : (s + 1) * PANEL]
        if r < ROWS - 1:
            value = nt(left(r + 1, 0, 2), full[r + 1].reshape(BLOCK, LANES)[:, :BLOCK])
        else:
            value = jnp.dot(
                left(r + 1, 0, 2), full[ROWS].reshape(BLOCK, LANES), preferred_element_type=F32
            )[:, :BLOCK]
        for s in range(2):
            acc[s + 1, :, :BLOCK] += value[s * PANEL : (s + 1) * PANEL]
        for s in range(3):
            prod = acc[s]
            value = prod + twice * (lefts[r + 1][s].astype(F32) - prod)
            fresh[s, :, r * MAIN : (r + 1) * MAIN] = value[:, :MAIN].astype(BF16)
            tail = value[:, MAIN:BLOCK].astype(BF16)
            for q, (low, high) in enumerate(INNER_QUARTERS):
                begin, end = max(low, s * PANEL), min(high, (s + 1) * PANEL)
                if begin < end:
                    lane = r * 256 + q * ATOMS
                    last[begin - low : end - low, lane : lane + ATOMS] = tail[
                        begin - s * PANEL : end - s * PANEL
                    ]
    rems = []
    for g in range(2):
        main, rem = deal(quad, fresh, g, 3)
        out[:, g * 384 : (g + 1) * 384] = main.astype(BF16)
        rems.append(rem)
    rems.append(nt(quad[...], last[...]))
    rems.append(jnp.zeros((1024, 32), F32))
    out[:, 768:] = jnp.concatenate(rems, axis=1).astype(BF16)


def unpack_outer_kernel(z, spread, out, held, sems):
    copies = []

    def send(o, s, high):
        row = s * 4 * PANEL
        copies.append(
            pltpu.make_async_copy(
                held.at[o, s, :high], out.at[o, row : row + high], sems.at[len(copies)]
            )
        )
        copies[-1].start()

    rest = tn(z[:, 512:], spread[...]).astype(BF16)
    for q in range(4):
        piece = rest[64:, q * 256 : (q + 1) * 256]
        held[8, q // 2, (q % 2) * 64 : (q % 2) * 64 + 64, :] = piece
    for s in range(2):
        send(8, s, 128)
    for g in range(2):
        main = tn(z[:, g * 256 : (g + 1) * 256], spread[...]).astype(BF16)
        for q in range(4):
            for s in range(2):
                lanes = slice(q * 256, (q + 1) * 256)
                held[4 * g + q, s, :128, :] = main[s * 128 : (s + 1) * 128, lanes]
                begin = g * 32 + s * 16
                held[4 * g + q, s, 128:, :] = rest[begin : begin + 16, lanes]
                send(4 * g + q, s, PANEL)
    for copy in copies:
        copy.wait()


def unpack_inner_kernel(z, spread, begun, out, held, edge, sems):
    del begun
    copies = []

    def send(src, dst):
        copies.append(pltpu.make_async_copy(src, dst, sems.at[len(copies)]))
        copies[-1].start()

    rest = tn(z[:, 768:], spread[...]).astype(BF16)
    for q, (low, high) in enumerate(INNER_QUARTERS):
        held[8, low:high, :] = rest[96 : 96 + high - low, q * 256 : (q + 1) * 256]
    send(held.at[8], out.at[8, PANEL : 4 * PANEL])
    for s in range(2):
        edge[s] = rest[208:224, s * 256 : (s + 1) * 256]
        row = s * 4 * PANEL + 128
        send(edge.at[s], out.at[8, row : row + 16])
    for g in range(2):
        main = tn(z[:, g * 384 : (g + 1) * 384], spread[...]).astype(BF16)
        for q in range(4):
            for s in range(3):
                lanes = slice(q * 256, (q + 1) * 256)
                held[4 * g + q, s * PANEL : s * PANEL + 128, :] = main[s * 128 : (s + 1) * 128, lanes]
                begin = g * 48 + s * 16
                held[4 * g + q, s * PANEL + 128 : (s + 1) * PANEL, :] = rest[begin : begin + 16, lanes]
            send(held.at[4 * g + q], out.at[4 * g + q, PANEL : 4 * PANEL])
    for copy in copies:
        copy.wait()


def spread_matrix():
    w, q, j = np.meshgrid(np.arange(64), np.arange(4), np.arange(4), indexing="ij")
    table = np.zeros((1024, 1024), np.float32)
    table[np.arange(1024), (q * 256 + w * 4 + j).reshape(-1)] = 1.0
    return table


def shift_perm(count, step):
    return [(i, (i - step) % count) for i in range(count)]


def gather(own):
    return [own] + [lax.ppermute(own, "narrow", shift_perm(NARROW, step)) for step in (1, 2, 3)]


def narrow_sum(value):
    first, *others = gather(value)
    return first + others[0] + others[1] + others[2]


def wide_copies(value):
    copies = jnp.broadcast_to(value.reshape(1, 1, 128), (WIDE, 1, 128))
    return lax.all_to_all(copies, "wide", split_axis=0, concat_axis=0, tiled=True)


def exchange(packed, chunk):
    parts = packed.reshape(WIDE, 16, chunk)
    got = lax.all_to_all(parts, "wide", split_axis=0, concat_axis=0, tiled=True)
    return got.reshape(1024, chunk)


def shards(xblk, link, order):
    rows_total = link.shape[0]
    x = jnp.transpose(xblk, (0, 2, 1, 3))
    traces = pl.pallas_call(
        trace_kernel,
        out_shape=sds((1, 128), F32),
        in_specs=[SM, VM],
        out_specs=VM,
        compiler_params=params(),
        name="traces",
    )(link, x)
    line = narrow_sum(traces)
    sums = wide_copies(line)
    ga, gb, a_first, a_mid, a_last = pl.pallas_call(
        prep_kernel,
        out_shape=[
            sds((PANEL, 2944), BF16),
            sds((PANEL, 2304), BF16),
            sds((3, PANEL, LANES), BF16),
            sds((2, 3, PANEL, LANES), BF16),
            sds((3, PANEL, LANES), BF16),
        ],
        in_specs=[SM, VM, ANY],
        out_specs=[VM] * 5,
        compiler_params=params(),
        name="prep",
    )(link, x, traces)
    ga, a_first, a_last, _ = lax.optimization_barrier((ga, a_first, a_last, line))
    gas = gather(ga)
    a_prev = lax.ppermute(a_last, "wide", shift_perm(WIDE, -1))
    a_next = lax.ppermute(a_first, "wide", shift_perm(WIDE, 1))
    wanted = jnp.broadcast_to(order.reshape(64, 1, 4), (64, 4, 4))
    quarter = jnp.arange(4, dtype=jnp.int32).reshape(1, 4, 1)
    wanted = ((wanted // ATOMS) * 256 + quarter * ATOMS + wanted % ATOMS).reshape(1024, 1)
    quad = pl.pallas_call(
        deal_kernel,
        out_shape=sds((1024, 1024), BF16),
        in_specs=[VM],
        out_specs=VM,
        compiler_params=params(),
        name="deal",
    )(wanted)
    gb, sums, quad, a_prev, a_next, *gas = lax.optimization_barrier(
        (gb, sums, quad, a_prev, a_next, *gas)
    )
    gbs = gather(gb)
    lefts = (a_prev, a_first, a_mid, a_last, a_next)
    packed_outer, left_over = pl.pallas_call(
        lambda *refs: outer_kernel(rows_total, *refs),
        out_shape=[sds((1024, OUTER_CHUNK), BF16), sds((16, 1024), BF16)],
        in_specs=[VM] * 11,
        out_specs=[VM, VM],
        scratch_shapes=[
            pltpu.VMEM((ROWS + 1, ORB, NARROW, 16, LANES), BF16),
            pltpu.VMEM((2, PANEL, ROWS * MAIN), BF16),
            pltpu.VMEM((64, 1024), BF16),
        ],
        compiler_params=params(),
        cost_estimate=pl.CostEstimate(
            flops=OUTER_FLOPS, bytes_accessed=8 << 20, transcendentals=0
        ),
        name="outer",
    )(sums, *gas, *lefts, quad)
    got_outer = exchange(packed_outer, OUTER_CHUNK)
    packed_inner = pl.pallas_call(
        lambda *refs: inner_kernel(rows_total, *refs),
        out_shape=sds((1024, INNER_CHUNK), BF16),
        in_specs=[VM] * 16,
        out_specs=VM,
        scratch_shapes=[
            pltpu.VMEM((2 * ROWS + 1, ORB, NARROW, 16, LANES), BF16),
            pltpu.VMEM((3, PANEL, LANES), F32),
            pltpu.VMEM((3, PANEL, ROWS * MAIN), BF16),
            pltpu.VMEM((128, 1024), BF16),
        ],
        compiler_params=params(),
        cost_estimate=pl.CostEstimate(
            flops=INNER_FLOPS, bytes_accessed=12 << 20, transcendentals=0
        ),
        name="inner",
    )(sums, *gas, *gbs, *lefts, quad, left_over)
    packed_inner, got_outer = lax.optimization_barrier((packed_inner, got_outer))
    got_inner = exchange(packed_inner, INNER_CHUNK)
    spread = jnp.asarray(spread_matrix(), BF16)
    out = pl.pallas_call(
        unpack_outer_kernel,
        out_shape=sds((ORB, 5 * PANEL, 256), BF16),
        in_specs=[VM, VM],
        out_specs=ANY,
        scratch_shapes=[
            pltpu.VMEM((ORB, 2, PANEL, 256), BF16),
            pltpu.SemaphoreType.DMA((18,)),
        ],
        compiler_params=params(),
        name="unpack_outer",
    )(got_outer, spread)
    out = pl.pallas_call(
        unpack_inner_kernel,
        out_shape=sds((ORB, 5 * PANEL, 256), BF16),
        in_specs=[VM, VM, ANY],
        out_specs=ANY,
        scratch_shapes=[
            pltpu.VMEM((ORB, 3 * PANEL, 256), BF16),
            pltpu.VMEM((2, 16, 256), BF16),
            pltpu.SemaphoreType.DMA((11,)),
        ],
        input_output_aliases={2: 0},
        compiler_params=params(),
        name="unpack_inner",
    )(got_inner, spread, out)
    return out.reshape(ORB, 5, PANEL, 256)


def solution(mesh):
    return jax.shard_map(
        shards,
        mesh=mesh,
        in_specs=(P(None, "narrow", None, "wide"), P(), P("wide")),
        out_specs=P(None, None, "narrow", "wide"),
        check_vma=False,
    )
```

```python
import jax
import jax.numpy as jnp
import numpy as np
from jax import lax
from jax.experimental import pallas as pl
from jax.experimental.pallas import tpu as pltpu
from jax.sharding import PartitionSpec as P

ORB = 9
ATOMS = 64
BLOCK = 576
PANEL = 144
LANES = 640
ROWS = 4
NARROW = 4
WIDE = 64
MAIN = 512
OUTER_CHUNK = 640
INNER_CHUNK = 1024
INNER_QUARTERS = ((0, 112), (112, 224), (224, 336), (336, 432))
F32 = jnp.float32
BF16 = jnp.bfloat16
OUTER_FLOPS = 30 * 10**9
INNER_FLOPS = 70 * 10**9

VM = pl.BlockSpec(memory_space=pltpu.VMEM)
SM = pl.BlockSpec(memory_space=pltpu.SMEM)
ANY = pl.BlockSpec(memory_space=pl.ANY)
sds = jax.ShapeDtypeStruct


def params(mib):
    return pltpu.CompilerParams(vmem_limit_bytes=mib << 20)


def lane_mask(link, first, shift):
    lanes = lax.broadcasted_iota(jnp.int32, (1, ROWS * ATOMS), 1) // ATOMS
    total = link.shape[0]
    mask = jnp.zeros((1, ROWS * ATOMS), F32)
    for r in range(ROWS):
        value = link[lax.rem(first + (r + shift + total), total)].astype(F32)
        mask = jnp.where(lanes == r, value, mask)
    return mask


def reorder_matrix():
    i = lax.broadcasted_iota(jnp.int32, (PANEL, PANEL), 0)
    c = lax.broadcasted_iota(jnp.int32, (PANEL, PANEL), 1)
    return jnp.where(c == (i % 16) * ORB + i // 16, 1.0, 0.0).astype(BF16)


def packed_row(tiles, r, pad):
    parts = [t[:, r * ATOMS : (r + 1) * ATOMS] for t in tiles]
    if pad:
        parts.append(jnp.zeros((PANEL, ATOMS), BF16))
    return jnp.concatenate(parts, axis=1)


def put_panel(out, count, p, value):
    out[:, p * MAIN : (p + 1) * MAIN] = value[:, :MAIN]
    tail = count * MAIN + p * ATOMS
    out[:, tail : tail + ATOMS] = value[:, MAIN:BLOCK]


def prep_outer_kernel(link, low, high, ga):
    first = lax.axis_index("wide") * ROWS
    before = lane_mask(link, first, -1).astype(BF16)
    after = lane_mask(link, first, 0).astype(BF16)
    reorder = reorder_matrix()
    tiles = [low[0, o] * before for o in range(ORB)]
    for p in range(ROWS + 1):
        if p == ROWS:
            tiles = [high[0, o] * after for o in range(ORB)]
        value = packed_row(tiles, min(p, ROWS - 1), False)
        turned = jnp.dot(reorder, value, preferred_element_type=F32).astype(BF16)
        put_panel(ga, ROWS + 1, p, turned)
    ga[:, (ROWS + 1) * BLOCK :] = jnp.zeros((PANEL, ATOMS), BF16)


def prep_inner_kernel(link, x, ga, gb, a_first, a_mid, a_last, traces):
    del ga
    first = lax.axis_index("wide") * ROWS
    masks = (lane_mask(link, first, -1), None, lane_mask(link, first, 0))
    squares = jnp.zeros((PANEL, ROWS * ATOMS), F32)
    for j in range(3):
        total = jnp.zeros((PANEL, ROWS * ATOMS), F32)
        for o in range(ORB):
            t = x[j, o].astype(F32)
            total = total + t * t
        if masks[j] is not None:
            total = total * masks[j]
        squares = squares + total
    narrow = lax.axis_index("narrow")
    rows = lax.broadcasted_iota(jnp.int32, (PANEL, ROWS * ATOMS), 0) + narrow * PANEL
    lanes = lax.broadcasted_iota(jnp.int32, (PANEL, ROWS * ATOMS), 1) % ATOMS
    diagonal = jnp.zeros((PANEL, ROWS * ATOMS), F32)
    for o in range(ORB):
        diagonal = diagonal + jnp.where(rows == lanes * ORB + o, x[1, o].astype(F32), 0.0)
    sq = jnp.sum(squares, axis=0, keepdims=True)
    tx = jnp.sum(diagonal, axis=0, keepdims=True)
    sq = jnp.sum(sq, axis=1, keepdims=True)
    tx = jnp.sum(tx, axis=1, keepdims=True)
    lane = lax.broadcasted_iota(jnp.int32, (1, 128), 1)
    value = jnp.where(lane == 0, tx, jnp.where(lane == 1, sq, 0.0))
    traces[...] = jnp.broadcast_to(value.reshape(1, 1, 128), (WIDE, 1, 128))
    reorder = reorder_matrix()
    for j in range(3):
        tiles = [x[j, o] for o in range(ORB)]
        if masks[j] is not None:
            tiles = [t * masks[j].astype(BF16) for t in tiles]
        for r in range(ROWS):
            value = packed_row(tiles, r, True)
            if r == 0:
                a_first[j] = value
            elif r == ROWS - 1:
                a_last[j] = value
            else:
                a_mid[r - 1, j] = value
            if j == 1:
                turned = jnp.dot(reorder, value, preferred_element_type=F32).astype(BF16)
                put_panel(gb, ROWS, r, turned)


def deal_kernel(wanted, quad):
    step = 128
    for k in range(0, 1024, step):
        lanes = lax.broadcasted_iota(jnp.int32, (step, 1024), 1)
        quad[k : k + step, :] = jnp.where(lanes == wanted[k : k + step, :], 1.0, 0.0).astype(BF16)


def nt(a, b):
    return lax.dot_general(a, b, (((1,), (1,)), ((), ())), preferred_element_type=F32)


def tn(a, b):
    return lax.dot_general(a, b, (((0,), (0,)), ((), ())), preferred_element_type=F32)


def twice_weight(sums, rows_total):
    total = sums[0][...] + sums[1][...] + sums[2][...] + sums[3][...]
    tx = total[:, 0:1]
    sq = total[:, 1:2]
    return 2.0 * jax.nn.sigmoid(4.0 * (tx - sq) / (rows_total * BLOCK) + 5.0)


def assemble(full, base, count, sources):
    narrow = lax.axis_index("narrow")
    if len(sources) == NARROW:
        places = tuple((shift, 0, ORB) for shift in range(NARROW))
    else:
        places = ((0, 0, ORB), (1, 0, ORB), (2, 0, 5), (2, 5, 4), (3, 0, ORB))
    for (shift, o, depth), src in zip(places, sources):
        owner = lax.rem(narrow + shift, NARROW)
        for p in range(count):
            value = src[:, p * MAIN : (p + 1) * MAIN]
            full[base + p, o : o + depth, pl.ds(owner, 1), :, :MAIN] = value.reshape(
                depth, 1, 16, MAIN
            )
            tail = count * MAIN + p * ATOMS
            value = src[:, tail : tail + ATOMS]
            full[base + p, o : o + depth, pl.ds(owner, 1), :, MAIN:BLOCK] = value.reshape(
                depth, 1, 16, ATOMS
            )


def deal(quad, fresh, group, slabs):
    lanes = [slice(r * MAIN + group * 256, r * MAIN + group * 256 + 256) for r in range(ROWS)]
    main = jnp.concatenate([fresh[:, :128, l].reshape(slabs * 128, 256) for l in lanes], axis=1)
    rem = jnp.concatenate([fresh[:, 128:, l].reshape(slabs * 16, 256) for l in lanes], axis=1)
    return nt(quad[...], main), nt(quad[...], rem)


def outer_kernel(
    rows_total, sum0, sum1, sum2, sum3, ga0, ga1, ga2, ga3, ga4, a_prev, a_first, a_mid, a_last, a_next, quad,
    out, left_over, full, fresh, last,
):
    gas = (ga0, ga1, ga2, ga3, ga4)
    twice = twice_weight((sum0, sum1, sum2, sum3), rows_total)
    assemble(full, 0, ROWS + 1, gas)
    lefts = [a_prev, a_first, a_mid.at[0], a_mid.at[1], a_last, a_next]
    left_over[...] = jnp.zeros_like(left_over)
    for r in range(ROWS):
        for s in range(2):
            if s == 0:
                b = full[r].reshape(BLOCK, LANES)
                prod = jnp.dot(lefts[r][0][:, :BLOCK], b, preferred_element_type=F32)
            elif r < ROWS - 1:
                b = full[r + 1].reshape(BLOCK, LANES)[:, :BLOCK]
                prod = nt(lefts[r + 2][2][:, :BLOCK], b)
            else:
                b = full[ROWS].reshape(BLOCK, LANES)
                prod = jnp.dot(lefts[r + 2][2][:, :BLOCK], b, preferred_element_type=F32)
            value = prod + twice * (0.0 - prod)
            fresh[s, :, r * MAIN : (r + 1) * MAIN] = value[:, :MAIN].astype(BF16)
            tail = value[:, MAIN:BLOCK].astype(BF16)
            for half in range(2):
                lane = r * 256 + (2 * s + half) * ATOMS
                last[:, lane : lane + ATOMS] = tail[half * 64 : half * 64 + 64]
            lane = r * 256 + s * ATOMS
            left_over[:, lane : lane + ATOMS] = tail[128:]
    rems = []
    for g in range(2):
        main, rem = deal(quad, fresh, g, 2)
        out[:, g * 256 : (g + 1) * 256] = main.astype(BF16)
        rems.append(rem)
    rems.append(nt(quad[...], last[...]))
    out[:, 512:] = jnp.concatenate(rems, axis=1).astype(BF16)


def inner_kernel(
    rows_total, sum0, sum1, sum2, sum3, ga0, ga1, ga2, ga3, ga4, gb0, gb1, gb2, gb3,
    a_prev, a_first, a_mid, a_last, a_next, quad, left_over,
    out, full, acc, fresh, last,
):
    gas = (ga0, ga1, ga2, ga3, ga4)
    gbs = (gb0, gb1, gb2, gb3)
    twice = twice_weight((sum0, sum1, sum2, sum3), rows_total)
    assemble(full, 0, ROWS + 1, gas)
    assemble(full, ROWS + 1, ROWS, gbs)
    lefts = [a_prev, a_first, a_mid.at[0], a_mid.at[1], a_last, a_next]

    def left(r, low, high):
        return jnp.concatenate([lefts[r + 1][j][:, :BLOCK] for j in range(low, high)], axis=0)

    last[112:, :] = left_over[...]
    last[96:112, :] = jnp.zeros((16, 1024), BF16)
    for r in range(ROWS):
        value = jnp.dot(
            left(r, 0, 3), full[ROWS + 1 + r].reshape(BLOCK, LANES), preferred_element_type=F32
        )
        for s in range(3):
            acc[s] = value[s * PANEL : (s + 1) * PANEL]
        value = jnp.dot(
            left(r - 1, 1, 3), full[r].reshape(BLOCK, LANES), preferred_element_type=F32
        )
        for s in range(2):
            acc[s] += value[s * PANEL : (s + 1) * PANEL]
        if r < ROWS - 1:
            value = nt(left(r + 1, 0, 2), full[r + 1].reshape(BLOCK, LANES)[:, :BLOCK])
        else:
            value = jnp.dot(
                left(r + 1, 0, 2), full[ROWS].reshape(BLOCK, LANES), preferred_element_type=F32
            )[:, :BLOCK]
        for s in range(2):
            acc[s + 1, :, :BLOCK] += value[s * PANEL : (s + 1) * PANEL]
        for s in range(3):
            prod = acc[s]
            value = prod + twice * (lefts[r + 1][s].astype(F32) - prod)
            fresh[s, :, r * MAIN : (r + 1) * MAIN] = value[:, :MAIN].astype(BF16)
            tail = value[:, MAIN:BLOCK].astype(BF16)
            for q, (low, high) in enumerate(INNER_QUARTERS):
                begin, end = max(low, s * PANEL), min(high, (s + 1) * PANEL)
                if begin < end:
                    lane = r * 256 + q * ATOMS
                    last[begin - low : end - low, lane : lane + ATOMS] = tail[
                        begin - s * PANEL : end - s * PANEL
                    ]
    rems = []
    for g in range(2):
        main, rem = deal(quad, fresh, g, 3)
        out[:, g * 384 : (g + 1) * 384] = main.astype(BF16)
        rems.append(rem)
    rems.append(nt(quad[...], last[...]))
    rems.append(jnp.zeros((1024, 32), F32))
    out[:, 768:] = jnp.concatenate(rems, axis=1).astype(BF16)


def unpack_outer_kernel(z, spread, out, held, sems):
    copies = []

    def send(o, s, high):
        row = s * 4 * PANEL
        copies.append(
            pltpu.make_async_copy(
                held.at[o, s, :high], out.at[o, row : row + high], sems.at[len(copies)]
            )
        )
        copies[-1].start()

    rest = tn(z[:, 512:], spread[...]).astype(BF16)
    for q in range(4):
        piece = rest[64:, q * 256 : (q + 1) * 256]
        held[8, q // 2, (q % 2) * 64 : (q % 2) * 64 + 64, :] = piece
    for s in range(2):
        send(8, s, 128)
    for g in range(2):
        main = tn(z[:, g * 256 : (g + 1) * 256], spread[...]).astype(BF16)
        for q in range(4):
            for s in range(2):
                lanes = slice(q * 256, (q + 1) * 256)
                held[4 * g + q, s, :128, :] = main[s * 128 : (s + 1) * 128, lanes]
                begin = g * 32 + s * 16
                held[4 * g + q, s, 128:, :] = rest[begin : begin + 16, lanes]
                send(4 * g + q, s, PANEL)
    for copy in copies:
        copy.wait()


def unpack_inner_kernel(z, spread, begun, out, held, edge, sems):
    del begun
    copies = []

    def send(src, dst):
        copies.append(pltpu.make_async_copy(src, dst, sems.at[len(copies)]))
        copies[-1].start()

    rest = tn(z[:, 768:], spread[...]).astype(BF16)
    for q, (low, high) in enumerate(INNER_QUARTERS):
        held[8, low:high, :] = rest[96 : 96 + high - low, q * 256 : (q + 1) * 256]
    send(held.at[8], out.at[8, PANEL : 4 * PANEL])
    for s in range(2):
        edge[s] = rest[208:224, s * 256 : (s + 1) * 256]
        row = s * 4 * PANEL + 128
        send(edge.at[s], out.at[8, row : row + 16])
    for g in range(2):
        main = tn(z[:, g * 384 : (g + 1) * 384], spread[...]).astype(BF16)
        for q in range(4):
            for s in range(3):
                lanes = slice(q * 256, (q + 1) * 256)
                held[4 * g + q, s * PANEL : s * PANEL + 128, :] = main[s * 128 : (s + 1) * 128, lanes]
                begin = g * 48 + s * 16
                held[4 * g + q, s * PANEL + 128 : (s + 1) * PANEL, :] = rest[begin : begin + 16, lanes]
            send(held.at[4 * g + q], out.at[4 * g + q, PANEL : 4 * PANEL])
    for copy in copies:
        copy.wait()


def spread_matrix():
    w, q, j = np.meshgrid(np.arange(64), np.arange(4), np.arange(4), indexing="ij")
    table = np.zeros((1024, 1024), np.float32)
    table[np.arange(1024), (q * 256 + w * 4 + j).reshape(-1)] = 1.0
    return table


def shift_perm(count, step):
    return [(i, (i - step) % count) for i in range(count)]


def neighbours(own):
    after = lax.ppermute(own, "narrow", shift_perm(NARROW, 1))
    before = lax.ppermute(own, "narrow", shift_perm(NARROW, -1))
    return after, before


def opposite(after, before):
    split = 80
    top, bottom = lax.optimization_barrier((after[:split], before[split:]))
    top = lax.ppermute(top, "narrow", shift_perm(NARROW, 1))
    bottom = lax.ppermute(bottom, "narrow", shift_perm(NARROW, -1))
    return top, bottom


def direct_gather(own):
    return [own] + [lax.ppermute(own, "narrow", shift_perm(NARROW, step)) for step in (1, 2, 3)]


def exchange(packed, chunk):
    parts = packed.reshape(WIDE, 16, chunk)
    got = lax.all_to_all(parts, "wide", split_axis=0, concat_axis=0, tiled=True)
    return got.reshape(1024, chunk)


def shards(xblk, link, order):
    rows_total = link.shape[0]
    x = jnp.transpose(xblk, (0, 2, 1, 3))
    slab = (1, ORB, PANEL, ROWS * ATOMS)
    ga = pl.pallas_call(
        prep_outer_kernel,
        out_shape=sds((PANEL, 2944), BF16),
        grid=(1,),
        in_specs=[
            SM,
            pl.BlockSpec(slab, lambda i: (0, 0, 0, 0)),
            pl.BlockSpec(slab, lambda i: (2, 0, 0, 0)),
        ],
        out_specs=pl.BlockSpec((PANEL, 2944), lambda i: (0, 0)),
        compiler_params=params(48),
        name="prep_outer",
    )(link, x, x)
    after, before = neighbours(ga)
    gb, a_first, a_mid, a_last, traces = pl.pallas_call(
        prep_inner_kernel,
        out_shape=[
            sds((PANEL, 2304), BF16),
            sds((3, PANEL, LANES), BF16),
            sds((2, 3, PANEL, LANES), BF16),
            sds((3, PANEL, LANES), BF16),
            sds((WIDE, 1, 128), F32),
        ],
        in_specs=[SM, VM, ANY],
        out_specs=[VM] * 5,
        compiler_params=params(48),
        name="prep_inner",
    )(link, x, ga)
    a_prev = lax.ppermute(a_last, "wide", shift_perm(WIDE, -1))
    a_next = lax.ppermute(a_first, "wide", shift_perm(WIDE, 1))
    line = lax.all_to_all(traces, "wide", split_axis=0, concat_axis=0, tiled=True)
    line = jnp.sum(line, axis=0)
    sums = direct_gather(line)
    after, before, a_prev, a_next = lax.optimization_barrier((after, before, a_prev, a_next))
    gas = (ga, after, *opposite(after, before), before)
    wanted = jnp.broadcast_to(order.reshape(64, 1, 4), (64, 4, 4))
    quarter = jnp.arange(4, dtype=jnp.int32).reshape(1, 4, 1)
    wanted = ((wanted // ATOMS) * 256 + quarter * ATOMS + wanted % ATOMS).reshape(1024, 1)
    quad = pl.pallas_call(
        deal_kernel,
        out_shape=sds((1024, 1024), BF16),
        in_specs=[VM],
        out_specs=VM,
        compiler_params=params(8),
        name="deal",
    )(wanted)
    gb, quad, a_prev, a_next, sums, gas = lax.optimization_barrier(
        (gb, quad, a_prev, a_next, sums, gas)
    )
    gbs = direct_gather(gb)
    lefts = (a_prev, a_first, a_mid, a_last, a_next)
    packed_outer, left_over = pl.pallas_call(
        lambda *refs: outer_kernel(rows_total, *refs),
        out_shape=[sds((1024, OUTER_CHUNK), BF16), sds((16, 1024), BF16)],
        in_specs=[VM] * 15,
        out_specs=[VM, VM],
        scratch_shapes=[
            pltpu.VMEM((ROWS + 1, ORB, NARROW, 16, LANES), BF16),
            pltpu.VMEM((2, PANEL, ROWS * MAIN), BF16),
            pltpu.VMEM((64, 1024), BF16),
        ],
        compiler_params=params(24),
        cost_estimate=pl.CostEstimate(
            flops=OUTER_FLOPS, bytes_accessed=8 << 20, transcendentals=0
        ),
        name="outer",
    )(*sums, *gas, *lefts, quad)
    got_outer = exchange(packed_outer, OUTER_CHUNK)
    packed_inner = pl.pallas_call(
        lambda *refs: inner_kernel(rows_total, *refs),
        out_shape=sds((1024, INNER_CHUNK), BF16),
        in_specs=[VM] * 20,
        out_specs=VM,
        scratch_shapes=[
            pltpu.VMEM((2 * ROWS + 1, ORB, NARROW, 16, LANES), BF16),
            pltpu.VMEM((3, PANEL, LANES), F32),
            pltpu.VMEM((3, PANEL, ROWS * MAIN), BF16),
            pltpu.VMEM((128, 1024), BF16),
        ],
        compiler_params=params(54),
        cost_estimate=pl.CostEstimate(
            flops=INNER_FLOPS, bytes_accessed=12 << 20, transcendentals=0
        ),
        name="inner",
    )(*sums, *gas, *gbs, *lefts, quad, left_over)
    packed_inner, got_outer = lax.optimization_barrier((packed_inner, got_outer))
    got_inner = exchange(packed_inner, INNER_CHUNK)
    spread = jnp.asarray(spread_matrix(), BF16)
    out = pl.pallas_call(
        unpack_outer_kernel,
        out_shape=sds((ORB, 5 * PANEL, 256), BF16),
        in_specs=[VM, VM],
        out_specs=ANY,
        scratch_shapes=[
            pltpu.VMEM((ORB, 2, PANEL, 256), BF16),
            pltpu.SemaphoreType.DMA((18,)),
        ],
        compiler_params=params(14),
        name="unpack_outer",
    )(got_outer, spread)
    out = pl.pallas_call(
        unpack_inner_kernel,
        out_shape=sds((ORB, 5 * PANEL, 256), BF16),
        in_specs=[VM, VM, ANY],
        out_specs=ANY,
        scratch_shapes=[
            pltpu.VMEM((ORB, 3 * PANEL, 256), BF16),
            pltpu.VMEM((2, 16, 256), BF16),
            pltpu.SemaphoreType.DMA((11,)),
        ],
        input_output_aliases={2: 0},
        compiler_params=params(16),
        name="unpack_inner",
    )(got_inner, spread, out)
    return out.reshape(ORB, 5, PANEL, 256)


def solution(mesh):
    return jax.shard_map(
        shards,
        mesh=mesh,
        in_specs=(P(None, "narrow", None, "wide"), P(), P("wide")),
        out_specs=P(None, None, "narrow", "wide"),
        check_vma=False,
    )
```

```python
import jax
import jax.numpy as jnp
import numpy as np
from jax import lax
from jax.experimental import pallas as pl
from jax.experimental.pallas import tpu as pltpu
from jax.sharding import PartitionSpec as P

ORB = 9
ATOMS = 64
BLOCK = 576
PANEL = 144
LANES = 640
ROWS = 4
NARROW = 4
WIDE = 64
MAIN = 512
OUTER_CHUNK = 640
INNER_CHUNK = 1024
INNER_QUARTERS = ((0, 112), (112, 224), (224, 336), (336, 432))
F32 = jnp.float32
BF16 = jnp.bfloat16
OUTER_FLOPS = 30 * 10**9
INNER_FLOPS = 70 * 10**9

VM = pl.BlockSpec(memory_space=pltpu.VMEM)
SM = pl.BlockSpec(memory_space=pltpu.SMEM)
ANY = pl.BlockSpec(memory_space=pl.ANY)
sds = jax.ShapeDtypeStruct


def params(mib):
    return pltpu.CompilerParams(vmem_limit_bytes=mib << 20)


def lane_mask(link, first, shift):
    lanes = lax.broadcasted_iota(jnp.int32, (1, ROWS * ATOMS), 1) // ATOMS
    total = link.shape[0]
    mask = jnp.zeros((1, ROWS * ATOMS), F32)
    for r in range(ROWS):
        value = link[lax.rem(first + (r + shift + total), total)].astype(F32)
        mask = jnp.where(lanes == r, value, mask)
    return mask


def reorder_matrix():
    i = lax.broadcasted_iota(jnp.int32, (PANEL, PANEL), 0)
    c = lax.broadcasted_iota(jnp.int32, (PANEL, PANEL), 1)
    return jnp.where(c == (i % 16) * ORB + i // 16, 1.0, 0.0).astype(BF16)


def packed_row(tiles, r, pad):
    parts = [t[:, r * ATOMS : (r + 1) * ATOMS] for t in tiles]
    if pad:
        parts.append(jnp.zeros((PANEL, ATOMS), BF16))
    return jnp.concatenate(parts, axis=1)


def put_panel(out, count, p, value):
    out[:, p * MAIN : (p + 1) * MAIN] = value[:, :MAIN]
    tail = count * MAIN + p * ATOMS
    out[:, tail : tail + ATOMS] = value[:, MAIN:BLOCK]


def prep_outer_kernel(link, low, high, ga):
    first = lax.axis_index("wide") * ROWS
    before = lane_mask(link, first, -1).astype(BF16)
    after = lane_mask(link, first, 0).astype(BF16)
    reorder = reorder_matrix()
    tiles = [low[0, o] * before for o in range(ORB)]
    for p in range(ROWS + 1):
        if p == ROWS:
            tiles = [high[0, o] * after for o in range(ORB)]
        value = packed_row(tiles, min(p, ROWS - 1), False)
        turned = jnp.dot(reorder, value, preferred_element_type=F32).astype(BF16)
        put_panel(ga, ROWS + 1, p, turned)
    ga[:, (ROWS + 1) * BLOCK :] = jnp.zeros((PANEL, ATOMS), BF16)


def prep_inner_kernel(link, x, ga, gb, a_first, a_mid, a_last, traces):
    del ga
    first = lax.axis_index("wide") * ROWS
    masks = (lane_mask(link, first, -1), None, lane_mask(link, first, 0))
    squares = jnp.zeros((PANEL, ROWS * ATOMS), F32)
    for j in range(3):
        total = jnp.zeros((PANEL, ROWS * ATOMS), F32)
        for o in range(ORB):
            t = x[j, o].astype(F32)
            total = total + t * t
        if masks[j] is not None:
            total = total * masks[j]
        squares = squares + total
    narrow = lax.axis_index("narrow")
    rows = lax.broadcasted_iota(jnp.int32, (PANEL, ROWS * ATOMS), 0) + narrow * PANEL
    lanes = lax.broadcasted_iota(jnp.int32, (PANEL, ROWS * ATOMS), 1) % ATOMS
    diagonal = jnp.zeros((PANEL, ROWS * ATOMS), F32)
    for o in range(ORB):
        diagonal = diagonal + jnp.where(rows == lanes * ORB + o, x[1, o].astype(F32), 0.0)
    sq = jnp.sum(squares, axis=0, keepdims=True)
    tx = jnp.sum(diagonal, axis=0, keepdims=True)
    sq = jnp.sum(sq, axis=1, keepdims=True)
    tx = jnp.sum(tx, axis=1, keepdims=True)
    lane = lax.broadcasted_iota(jnp.int32, (1, 128), 1)
    value = jnp.where(lane == 0, tx, jnp.where(lane == 1, sq, 0.0))
    traces[...] = jnp.broadcast_to(value.reshape(1, 1, 128), (WIDE, 1, 128))
    reorder = reorder_matrix()
    for j in range(3):
        tiles = [x[j, o] for o in range(ORB)]
        if masks[j] is not None:
            tiles = [t * masks[j].astype(BF16) for t in tiles]
        for r in range(ROWS):
            value = packed_row(tiles, r, True)
            if r == 0:
                a_first[j] = value
            elif r == ROWS - 1:
                a_last[j] = value
            else:
                a_mid[r - 1, j] = value
            if j == 1:
                turned = jnp.dot(reorder, value, preferred_element_type=F32).astype(BF16)
                put_panel(gb, ROWS, r, turned)


def deal_kernel(wanted, quad):
    step = 128
    for k in range(0, 1024, step):
        lanes = lax.broadcasted_iota(jnp.int32, (step, 1024), 1)
        quad[k : k + step, :] = jnp.where(lanes == wanted[k : k + step, :], 1.0, 0.0).astype(BF16)


def nt(a, b):
    return lax.dot_general(a, b, (((1,), (1,)), ((), ())), preferred_element_type=F32)


def tn(a, b):
    return lax.dot_general(a, b, (((0,), (0,)), ((), ())), preferred_element_type=F32)


def twice_weight(sums, rows_total):
    total = sums[0][...] + sums[1][...] + sums[2][...] + sums[3][...]
    tx = total[:, 0:1]
    sq = total[:, 1:2]
    return 2.0 * jax.nn.sigmoid(4.0 * (tx - sq) / (rows_total * BLOCK) + 5.0)


def assemble(full, base, count, sources):
    narrow = lax.axis_index("narrow")
    if len(sources) == NARROW:
        places = tuple((shift, 0, ORB) for shift in range(NARROW))
    else:
        places = ((0, 0, ORB), (1, 0, ORB), (2, 0, 5), (2, 5, 4), (3, 0, ORB))
    for (shift, o, depth), src in zip(places, sources):
        owner = lax.rem(narrow + shift, NARROW)
        for p in range(count):
            value = src[:, p * MAIN : (p + 1) * MAIN]
            full[base + p, o : o + depth, pl.ds(owner, 1), :, :MAIN] = value.reshape(
                depth, 1, 16, MAIN
            )
            tail = count * MAIN + p * ATOMS
            value = src[:, tail : tail + ATOMS]
            full[base + p, o : o + depth, pl.ds(owner, 1), :, MAIN:BLOCK] = value.reshape(
                depth, 1, 16, ATOMS
            )


def put_fresh(rows, value, r, s, slabs):
    for g in range(2):
        piece = value[:, g * 256 : (g + 1) * 256].astype(BF16)
        lanes = slice(r * 256, (r + 1) * 256)
        begin = (g * slabs + s) * 128
        rows[begin : begin + 128, lanes] = piece[:128]
        begin = slabs * 256 + (g * slabs + s) * 16
        rows[begin : begin + 16, lanes] = piece[128:]


def outer_kernel(
    rows_total, sum0, sum1, sum2, sum3, ga0, ga1, ga2, ga3, ga4,
    a_prev, a_first, a_mid, a_last, a_next, quad,
    out, left_over, full, rows,
):
    gas = (ga0, ga1, ga2, ga3, ga4)
    twice = twice_weight((sum0, sum1, sum2, sum3), rows_total)
    assemble(full, 0, ROWS + 1, gas)
    lefts = [a_prev, a_first, a_mid.at[0], a_mid.at[1], a_last, a_next]
    left_over[...] = jnp.zeros_like(left_over)
    for r in range(ROWS):
        for s in range(2):
            if s == 0:
                b = full[r].reshape(BLOCK, LANES)
                prod = jnp.dot(lefts[r][0][:, :BLOCK], b, preferred_element_type=F32)
            elif r < ROWS - 1:
                b = full[r + 1].reshape(BLOCK, LANES)[:, :BLOCK]
                prod = nt(lefts[r + 2][2][:, :BLOCK], b)
            else:
                b = full[ROWS].reshape(BLOCK, LANES)
                prod = jnp.dot(lefts[r + 2][2][:, :BLOCK], b, preferred_element_type=F32)
            value = prod + twice * (0.0 - prod)
            put_fresh(rows, value, r, s, 2)
            tail = value[:, MAIN:BLOCK].astype(BF16)
            for half in range(2):
                lane = r * 256 + (2 * s + half) * ATOMS
                rows[576:640, lane : lane + ATOMS] = tail[half * 64 : half * 64 + 64]
            lane = r * 256 + s * ATOMS
            left_over[:, lane : lane + ATOMS] = tail[128:]
    for k in range(0, 1024, 256):
        out[k : k + 256, :] = nt(quad[k : k + 256, :], rows[...]).astype(BF16)


def inner_kernel(
    rows_total, sum0, sum1, sum2, sum3, ga0, ga1, ga2, ga3, ga4, gb0, gb1, gb2, gb3,
    a_prev, a_first, a_mid, a_last, a_next, quad, left_over,
    out, full, acc, rows,
):
    gas = (ga0, ga1, ga2, ga3, ga4)
    gbs = (gb0, gb1, gb2, gb3)
    twice = twice_weight((sum0, sum1, sum2, sum3), rows_total)
    assemble(full, 0, ROWS + 1, gas)
    assemble(full, ROWS + 1, ROWS, gbs)
    lefts = [a_prev, a_first, a_mid.at[0], a_mid.at[1], a_last, a_next]

    def left(r, low, high):
        return jnp.concatenate([lefts[r + 1][j][:, :BLOCK] for j in range(low, high)], axis=0)

    rows[960:976, :] = jnp.zeros((16, 1024), BF16)
    rows[976:992, :] = left_over[...]
    rows[992:, :] = jnp.zeros((32, 1024), BF16)
    for r in range(ROWS):
        value = jnp.dot(
            left(r, 0, 3), full[ROWS + 1 + r].reshape(BLOCK, LANES), preferred_element_type=F32
        )
        for s in range(3):
            acc[s] = value[s * PANEL : (s + 1) * PANEL]
        value = jnp.dot(
            left(r - 1, 1, 3), full[r].reshape(BLOCK, LANES), preferred_element_type=F32
        )
        for s in range(2):
            acc[s] += value[s * PANEL : (s + 1) * PANEL]
        if r < ROWS - 1:
            value = nt(left(r + 1, 0, 2), full[r + 1].reshape(BLOCK, LANES)[:, :BLOCK])
        else:
            value = jnp.dot(
                left(r + 1, 0, 2), full[ROWS].reshape(BLOCK, LANES), preferred_element_type=F32
            )[:, :BLOCK]
        for s in range(2):
            acc[s + 1, :, :BLOCK] += value[s * PANEL : (s + 1) * PANEL]
        for s in range(3):
            prod = acc[s]
            value = prod + twice * (lefts[r + 1][s].astype(F32) - prod)
            put_fresh(rows, value, r, s, 3)
            tail = value[:, MAIN:BLOCK].astype(BF16)
            for q, (low, high) in enumerate(INNER_QUARTERS):
                begin, end = max(low, s * PANEL), min(high, (s + 1) * PANEL)
                if begin < end:
                    lane = r * 256 + q * ATOMS
                    rows[864 + begin - low : 864 + end - low, lane : lane + ATOMS] = tail[
                        begin - s * PANEL : end - s * PANEL
                    ]
    for k in range(0, 1024, 256):
        out[k : k + 256, :] = nt(quad[k : k + 256, :], rows[...]).astype(BF16)


def spread_out(z, lanes, spread):
    for half in range(2):
        value = tn(z[half * 512 : (half + 1) * 512, lanes], spread[...]).astype(BF16)
        for q in range(4):
            yield q, slice(half * 128, (half + 1) * 128), value[:, q * 128 : (q + 1) * 128]


def unpack_outer_kernel(z, spread, out, held, sems):
    copies = []

    def send(o, s, high):
        row = s * 4 * PANEL
        copies.append(
            pltpu.make_async_copy(
                held.at[o, s, :high], out.at[o, row : row + high], sems.at[len(copies)]
            )
        )
        copies[-1].start()

    for q, lanes, value in spread_out(z, slice(512, 640), spread):
        held[8, q // 2, (q % 2) * 64 : (q % 2) * 64 + 64, lanes] = value[64:]
        for g in range(2):
            for s in range(2):
                begin = g * 32 + s * 16
                held[4 * g + q, s, 128:, lanes] = value[begin : begin + 16]
    for s in range(2):
        send(8, s, 128)
    for g in range(2):
        for q, lanes, value in spread_out(z, slice(g * 256, (g + 1) * 256), spread):
            for s in range(2):
                held[4 * g + q, s, :128, lanes] = value[s * 128 : (s + 1) * 128]
        for q in range(4):
            for s in range(2):
                send(4 * g + q, s, PANEL)
    for copy in copies:
        copy.wait()


def unpack_inner_kernel(z, spread, begun, out, held, edge, sems):
    del begun
    copies = []

    def send(src, dst):
        copies.append(pltpu.make_async_copy(src, dst, sems.at[len(copies)]))
        copies[-1].start()

    for q, lanes, value in spread_out(z, slice(768, 1024), spread):
        low, high = INNER_QUARTERS[q]
        held[8, low:high, lanes] = value[96 : 96 + high - low]
        if q < 2:
            edge[q, :, lanes] = value[208:224]
        for g in range(2):
            for s in range(3):
                begin = g * 48 + s * 16
                held[4 * g + q, s * PANEL + 128 : (s + 1) * PANEL, lanes] = value[
                    begin : begin + 16
                ]
    send(held.at[8], out.at[8, PANEL : 4 * PANEL])
    for s in range(2):
        row = s * 4 * PANEL + 128
        send(edge.at[s], out.at[8, row : row + 16])
    for g in range(2):
        for q, lanes, value in spread_out(z, slice(g * 384, (g + 1) * 384), spread):
            for s in range(3):
                held[4 * g + q, s * PANEL : s * PANEL + 128, lanes] = value[
                    s * 128 : (s + 1) * 128
                ]
        for q in range(4):
            send(held.at[4 * g + q], out.at[4 * g + q, PANEL : 4 * PANEL])
    for copy in copies:
        copy.wait()


def spread_matrix():
    w, q, j = np.meshgrid(np.arange(32), np.arange(4), np.arange(4), indexing="ij")
    table = np.zeros((512, 512), np.float32)
    table[np.arange(512), (q * 128 + w * 4 + j).reshape(-1)] = 1.0
    return table


def shift_perm(count, step):
    return [(i, (i - step) % count) for i in range(count)]


def neighbours(own):
    after = lax.ppermute(own, "narrow", shift_perm(NARROW, 1))
    before = lax.ppermute(own, "narrow", shift_perm(NARROW, -1))
    return after, before


def opposite(after, before):
    split = 80
    top, bottom = lax.optimization_barrier((after[:split], before[split:]))
    top = lax.ppermute(top, "narrow", shift_perm(NARROW, 1))
    bottom = lax.ppermute(bottom, "narrow", shift_perm(NARROW, -1))
    return top, bottom


def direct_gather(own):
    return [own] + [lax.ppermute(own, "narrow", shift_perm(NARROW, step)) for step in (1, 2, 3)]


def exchange(packed, chunk):
    parts = packed.reshape(WIDE, 16, chunk)
    got = lax.all_to_all(parts, "wide", split_axis=0, concat_axis=0, tiled=True)
    return got.reshape(1024, chunk)


def shards(xblk, link, order):
    rows_total = link.shape[0]
    x = jnp.transpose(xblk, (0, 2, 1, 3))
    slab = (1, ORB, PANEL, ROWS * ATOMS)
    ga = pl.pallas_call(
        prep_outer_kernel,
        out_shape=sds((PANEL, 2944), BF16),
        grid=(1,),
        in_specs=[
            SM,
            pl.BlockSpec(slab, lambda i: (0, 0, 0, 0)),
            pl.BlockSpec(slab, lambda i: (2, 0, 0, 0)),
        ],
        out_specs=pl.BlockSpec((PANEL, 2944), lambda i: (0, 0)),
        compiler_params=params(48),
        name="prep_outer",
    )(link, x, x)
    after, before = neighbours(ga)
    gb, a_first, a_mid, a_last, traces = pl.pallas_call(
        prep_inner_kernel,
        out_shape=[
            sds((PANEL, 2304), BF16),
            sds((3, PANEL, LANES), BF16),
            sds((2, 3, PANEL, LANES), BF16),
            sds((3, PANEL, LANES), BF16),
            sds((WIDE, 1, 128), F32),
        ],
        in_specs=[SM, VM, ANY],
        out_specs=[VM] * 5,
        compiler_params=params(48),
        name="prep_inner",
    )(link, x, ga)
    a_prev = lax.ppermute(a_last, "wide", shift_perm(WIDE, -1))
    a_next = lax.ppermute(a_first, "wide", shift_perm(WIDE, 1))
    line = lax.all_to_all(traces, "wide", split_axis=0, concat_axis=0, tiled=True)
    line = jnp.sum(line, axis=0)
    sums = direct_gather(line)
    after, before, a_prev, a_next = lax.optimization_barrier((after, before, a_prev, a_next))
    gas = (ga, after, *opposite(after, before), before)
    wanted = jnp.broadcast_to(order.reshape(64, 1, 4), (64, 4, 4))
    quarter = jnp.arange(4, dtype=jnp.int32).reshape(1, 4, 1)
    wanted = ((wanted // ATOMS) * 256 + quarter * ATOMS + wanted % ATOMS).reshape(1024, 1)
    quad = pl.pallas_call(
        deal_kernel,
        out_shape=sds((1024, 1024), BF16),
        in_specs=[VM],
        out_specs=VM,
        compiler_params=params(8),
        name="deal",
    )(wanted)
    gb, quad, a_prev, a_next, sums = lax.optimization_barrier((gb, quad, a_prev, a_next, sums))
    gbs = direct_gather(gb)
    lefts = (a_prev, a_first, a_mid, a_last, a_next)
    packed_outer, left_over = pl.pallas_call(
        lambda *refs: outer_kernel(rows_total, *refs),
        out_shape=[sds((1024, OUTER_CHUNK), BF16), sds((16, 1024), BF16)],
        in_specs=[VM] * 15,
        out_specs=[VM, VM],
        scratch_shapes=[
            pltpu.VMEM((ROWS + 1, ORB, NARROW, 16, LANES), BF16),
            pltpu.VMEM((OUTER_CHUNK, 1024), BF16),
        ],
        compiler_params=params(24),
        cost_estimate=pl.CostEstimate(
            flops=OUTER_FLOPS, bytes_accessed=8 << 20, transcendentals=0
        ),
        name="outer",
    )(*sums, *gas, *lefts, quad)
    got_outer = exchange(packed_outer, OUTER_CHUNK)
    packed_inner = pl.pallas_call(
        lambda *refs: inner_kernel(rows_total, *refs),
        out_shape=sds((1024, INNER_CHUNK), BF16),
        in_specs=[VM] * 20,
        out_specs=VM,
        scratch_shapes=[
            pltpu.VMEM((2 * ROWS + 1, ORB, NARROW, 16, LANES), BF16),
            pltpu.VMEM((3, PANEL, LANES), F32),
            pltpu.VMEM((INNER_CHUNK, 1024), BF16),
        ],
        compiler_params=params(54),
        cost_estimate=pl.CostEstimate(
            flops=INNER_FLOPS, bytes_accessed=12 << 20, transcendentals=0
        ),
        name="inner",
    )(*sums, *gas, *gbs, *lefts, quad, left_over)
    packed_inner, got_outer = lax.optimization_barrier((packed_inner, got_outer))
    got_inner = exchange(packed_inner, INNER_CHUNK)
    spread = jnp.asarray(spread_matrix(), BF16)
    out = pl.pallas_call(
        unpack_outer_kernel,
        out_shape=sds((ORB, 5 * PANEL, 256), BF16),
        in_specs=[VM, VM],
        out_specs=ANY,
        scratch_shapes=[
            pltpu.VMEM((ORB, 2, PANEL, 256), BF16),
            pltpu.SemaphoreType.DMA((18,)),
        ],
        compiler_params=params(14),
        name="unpack_outer",
    )(got_outer, spread)
    out = pl.pallas_call(
        unpack_inner_kernel,
        out_shape=sds((ORB, 5 * PANEL, 256), BF16),
        in_specs=[VM, VM, ANY],
        out_specs=ANY,
        scratch_shapes=[
            pltpu.VMEM((ORB, 3 * PANEL, 256), BF16),
            pltpu.VMEM((2, 16, 256), BF16),
            pltpu.SemaphoreType.DMA((11,)),
        ],
        input_output_aliases={2: 0},
        compiler_params=params(16),
        name="unpack_inner",
    )(got_inner, spread, out)
    return out.reshape(ORB, 5, PANEL, 256)


def solution(mesh):
    return jax.shard_map(
        shards,
        mesh=mesh,
        in_specs=(P(None, "narrow", None, "wide"), P(), P("wide")),
        out_specs=P(None, None, "narrow", "wide"),
        check_vma=False,
    )
```

```python
import jax
import jax.numpy as jnp
import numpy as np
from jax import lax
from jax.experimental import pallas as pl
from jax.experimental.pallas import tpu as pltpu
from jax.sharding import PartitionSpec as P

ORB = 9
ATOMS = 64
BLOCK = 576
PANEL = 144
LANES = 640
ROWS = 4
SPLIT = 80
NARROW = 4
WIDE = 64
MAIN = 512
OUTER_CHUNK = 640
INNER_CHUNK = 1024
INNER_QUARTERS = ((0, 112), (112, 224), (224, 336), (336, 432))
F32 = jnp.float32
BF16 = jnp.bfloat16
OUTER_FLOPS = 30 * 10**9
INNER_FLOPS = 70 * 10**9

VM = pl.BlockSpec(memory_space=pltpu.VMEM)
SM = pl.BlockSpec(memory_space=pltpu.SMEM)
ANY = pl.BlockSpec(memory_space=pl.ANY)
sds = jax.ShapeDtypeStruct


def params(mib):
    return pltpu.CompilerParams(vmem_limit_bytes=mib << 20)


def lane_mask(link, first, shift):
    lanes = lax.broadcasted_iota(jnp.int32, (1, ROWS * ATOMS), 1) // ATOMS
    total = link.shape[0]
    mask = jnp.zeros((1, ROWS * ATOMS), F32)
    for r in range(ROWS):
        value = link[lax.rem(first + (r + shift + total), total)].astype(F32)
        mask = jnp.where(lanes == r, value, mask)
    return mask


def reorder_matrix():
    i = lax.broadcasted_iota(jnp.int32, (PANEL, PANEL), 0)
    c = lax.broadcasted_iota(jnp.int32, (PANEL, PANEL), 1)
    return jnp.where(c == (i % 16) * ORB + i // 16, 1.0, 0.0).astype(BF16)


def packed_row(tiles, r, pad):
    parts = [t[:, r * ATOMS : (r + 1) * ATOMS] for t in tiles]
    if pad:
        parts.append(jnp.zeros((PANEL, ATOMS), BF16))
    return jnp.concatenate(parts, axis=1)


def put_panel(out, count, p, value):
    out[:, p * MAIN : (p + 1) * MAIN] = value[:, :MAIN]
    tail = count * MAIN + p * ATOMS
    out[:, tail : tail + ATOMS] = value[:, MAIN:BLOCK]


def prep_outer_kernel(link, low, high, top, bottom):
    first = lax.axis_index("wide") * ROWS
    before = lane_mask(link, first, -1).astype(BF16)
    after = lane_mask(link, first, 0).astype(BF16)
    reorder = reorder_matrix()
    tiles = [low[0, o] * before for o in range(ORB)]
    for p in range(ROWS + 1):
        if p == ROWS:
            tiles = [high[0, o] * after for o in range(ORB)]
        value = packed_row(tiles, min(p, ROWS - 1), False)
        turned = jnp.dot(reorder, value, preferred_element_type=F32).astype(BF16)
        put_panel(top, ROWS + 1, p, turned[:SPLIT])
        put_panel(bottom, ROWS + 1, p, turned[SPLIT:])
    top[:, (ROWS + 1) * BLOCK :] = jnp.zeros((SPLIT, ATOMS), BF16)
    bottom[:, (ROWS + 1) * BLOCK :] = jnp.zeros((PANEL - SPLIT, ATOMS), BF16)


def prep_inner_kernel(link, x, ga, gb, a_first, a_mid, a_last, traces):
    del ga
    first = lax.axis_index("wide") * ROWS
    masks = (lane_mask(link, first, -1), None, lane_mask(link, first, 0))
    squares = jnp.zeros((PANEL, ROWS * ATOMS), F32)
    for j in range(3):
        total = jnp.zeros((PANEL, ROWS * ATOMS), F32)
        for o in range(ORB):
            t = x[j, o].astype(F32)
            total = total + t * t
        if masks[j] is not None:
            total = total * masks[j]
        squares = squares + total
    narrow = lax.axis_index("narrow")
    rows = lax.broadcasted_iota(jnp.int32, (PANEL, ROWS * ATOMS), 0) + narrow * PANEL
    lanes = lax.broadcasted_iota(jnp.int32, (PANEL, ROWS * ATOMS), 1) % ATOMS
    diagonal = jnp.zeros((PANEL, ROWS * ATOMS), F32)
    for o in range(ORB):
        diagonal = diagonal + jnp.where(rows == lanes * ORB + o, x[1, o].astype(F32), 0.0)
    sq = jnp.sum(squares, axis=0, keepdims=True)
    tx = jnp.sum(diagonal, axis=0, keepdims=True)
    sq = jnp.sum(sq, axis=1, keepdims=True)
    tx = jnp.sum(tx, axis=1, keepdims=True)
    lane = lax.broadcasted_iota(jnp.int32, (1, 128), 1)
    value = jnp.where(lane == 0, tx, jnp.where(lane == 1, sq, 0.0))
    traces[...] = jnp.broadcast_to(value.reshape(1, 1, 128), (WIDE, 1, 128))
    reorder = reorder_matrix()
    for j in range(3):
        tiles = [x[j, o] for o in range(ORB)]
        if masks[j] is not None:
            tiles = [t * masks[j].astype(BF16) for t in tiles]
        for r in range(ROWS):
            value = packed_row(tiles, r, True)
            if r == 0:
                a_first[j] = value
            elif r == ROWS - 1:
                a_last[j] = value
            else:
                a_mid[r - 1, j] = value
            if j == 1:
                turned = jnp.dot(reorder, value, preferred_element_type=F32).astype(BF16)
                put_panel(gb, ROWS, r, turned)


def deal_kernel(wanted, quad):
    step = 128
    for k in range(0, 1024, step):
        lanes = lax.broadcasted_iota(jnp.int32, (step, 1024), 1)
        quad[k : k + step, :] = jnp.where(lanes == wanted[k : k + step, :], 1.0, 0.0).astype(BF16)


def nt(a, b):
    return lax.dot_general(a, b, (((1,), (1,)), ((), ())), preferred_element_type=F32)


def tn(a, b):
    return lax.dot_general(a, b, (((0,), (0,)), ((), ())), preferred_element_type=F32)


def twice_weight(sums, rows_total):
    total = sums[0][...] + sums[1][...] + sums[2][...] + sums[3][...]
    tx = total[:, 0:1]
    sq = total[:, 1:2]
    return 2.0 * jax.nn.sigmoid(4.0 * (tx - sq) / (rows_total * BLOCK) + 5.0)


def assemble(full, base, count, sources):
    narrow = lax.axis_index("narrow")
    if len(sources) == NARROW:
        places = tuple((shift, 0, ORB) for shift in range(NARROW))
    else:
        cut = SPLIT // 16
        places = tuple(
            (shift, o, depth)
            for shift in range(NARROW)
            for o, depth in ((0, cut), (cut, ORB - cut))
        )
    for (shift, o, depth), src in zip(places, sources):
        owner = lax.rem(narrow + shift, NARROW)
        for p in range(count):
            value = src[:, p * MAIN : (p + 1) * MAIN]
            full[base + p, o : o + depth, pl.ds(owner, 1), :, :MAIN] = value.reshape(
                depth, 1, 16, MAIN
            )
            tail = count * MAIN + p * ATOMS
            value = src[:, tail : tail + ATOMS]
            full[base + p, o : o + depth, pl.ds(owner, 1), :, MAIN:BLOCK] = value.reshape(
                depth, 1, 16, ATOMS
            )


def put_fresh(rows, value, r, s, slabs):
    for g in range(2):
        piece = value[:, g * 256 : (g + 1) * 256].astype(BF16)
        lanes = slice(r * 256, (r + 1) * 256)
        begin = (g * slabs + s) * 128
        rows[begin : begin + 128, lanes] = piece[:128]
        begin = slabs * 256 + (g * slabs + s) * 16
        rows[begin : begin + 16, lanes] = piece[128:]


def outer_kernel(
    rows_total, sum0, sum1, sum2, sum3, ga0, ga1, ga2, ga3, ga4, ga5, ga6, ga7,
    a_prev, a_first, a_mid, a_last, a_next, quad,
    out, left_over, full, rows,
):
    gas = (ga0, ga1, ga2, ga3, ga4, ga5, ga6, ga7)
    twice = twice_weight((sum0, sum1, sum2, sum3), rows_total)
    assemble(full, 0, ROWS + 1, gas)
    lefts = [a_prev, a_first, a_mid.at[0], a_mid.at[1], a_last, a_next]
    left_over[...] = jnp.zeros_like(left_over)
    for r in range(ROWS):
        for s in range(2):
            if s == 0:
                b = full[r].reshape(BLOCK, LANES)
                prod = jnp.dot(lefts[r][0][:, :BLOCK], b, preferred_element_type=F32)
            elif r < ROWS - 1:
                b = full[r + 1].reshape(BLOCK, LANES)[:, :BLOCK]
                prod = nt(lefts[r + 2][2][:, :BLOCK], b)
            else:
                b = full[ROWS].reshape(BLOCK, LANES)
                prod = jnp.dot(lefts[r + 2][2][:, :BLOCK], b, preferred_element_type=F32)
            value = prod + twice * (0.0 - prod)
            put_fresh(rows, value, r, s, 2)
            tail = value[:, MAIN:BLOCK].astype(BF16)
            for half in range(2):
                lane = r * 256 + (2 * s + half) * ATOMS
                rows[576:640, lane : lane + ATOMS] = tail[half * 64 : half * 64 + 64]
            lane = r * 256 + s * ATOMS
            left_over[:, lane : lane + ATOMS] = tail[128:]
    for k in range(0, 1024, 256):
        out[k : k + 256, :] = nt(quad[k : k + 256, :], rows[...]).astype(BF16)


def inner_kernel(
    rows_total, sum0, sum1, sum2, sum3, ga0, ga1, ga2, ga3, ga4, ga5, ga6, ga7, gb0, gb1, gb2, gb3,
    a_prev, a_first, a_mid, a_last, a_next, quad, left_over,
    out, full, acc, rows,
):
    gas = (ga0, ga1, ga2, ga3, ga4, ga5, ga6, ga7)
    gbs = (gb0, gb1, gb2, gb3)
    twice = twice_weight((sum0, sum1, sum2, sum3), rows_total)
    assemble(full, 0, ROWS + 1, gas)
    assemble(full, ROWS + 1, ROWS, gbs)
    lefts = [a_prev, a_first, a_mid.at[0], a_mid.at[1], a_last, a_next]

    def left(r, low, high):
        return jnp.concatenate([lefts[r + 1][j][:, :BLOCK] for j in range(low, high)], axis=0)

    rows[960:976, :] = jnp.zeros((16, 1024), BF16)
    rows[976:992, :] = left_over[...]
    rows[992:, :] = jnp.zeros((32, 1024), BF16)
    for r in range(ROWS):
        value = jnp.dot(
            left(r, 0, 3), full[ROWS + 1 + r].reshape(BLOCK, LANES), preferred_element_type=F32
        )
        for s in range(3):
            acc[s] = value[s * PANEL : (s + 1) * PANEL]
        value = jnp.dot(
            left(r - 1, 1, 3), full[r].reshape(BLOCK, LANES), preferred_element_type=F32
        )
        for s in range(2):
            acc[s] += value[s * PANEL : (s + 1) * PANEL]
        if r < ROWS - 1:
            value = nt(left(r + 1, 0, 2), full[r + 1].reshape(BLOCK, LANES)[:, :BLOCK])
        else:
            value = jnp.dot(
                left(r + 1, 0, 2), full[ROWS].reshape(BLOCK, LANES), preferred_element_type=F32
            )[:, :BLOCK]
        for s in range(2):
            acc[s + 1, :, :BLOCK] += value[s * PANEL : (s + 1) * PANEL]
        for s in range(3):
            prod = acc[s]
            value = prod + twice * (lefts[r + 1][s].astype(F32) - prod)
            put_fresh(rows, value, r, s, 3)
            tail = value[:, MAIN:BLOCK].astype(BF16)
            for q, (low, high) in enumerate(INNER_QUARTERS):
                begin, end = max(low, s * PANEL), min(high, (s + 1) * PANEL)
                if begin < end:
                    lane = r * 256 + q * ATOMS
                    rows[864 + begin - low : 864 + end - low, lane : lane + ATOMS] = tail[
                        begin - s * PANEL : end - s * PANEL
                    ]
    for k in range(0, 1024, 256):
        out[k : k + 256, :] = nt(quad[k : k + 256, :], rows[...]).astype(BF16)


def spread_out(z, lanes, spread):
    for half in range(2):
        value = tn(z[half * 512 : (half + 1) * 512, lanes], spread[...]).astype(BF16)
        for q in range(4):
            yield q, slice(half * 128, (half + 1) * 128), value[:, q * 128 : (q + 1) * 128]


def unpack_outer_kernel(z, spread, out, held, sems):
    copies = []

    def send(o, s, high):
        row = s * 4 * PANEL
        copies.append(
            pltpu.make_async_copy(
                held.at[o, s, :high], out.at[o, row : row + high], sems.at[len(copies)]
            )
        )
        copies[-1].start()

    for q, lanes, value in spread_out(z, slice(512, 640), spread):
        held[8, q // 2, (q % 2) * 64 : (q % 2) * 64 + 64, lanes] = value[64:]
        for g in range(2):
            for s in range(2):
                begin = g * 32 + s * 16
                held[4 * g + q, s, 128:, lanes] = value[begin : begin + 16]
    for s in range(2):
        send(8, s, 128)
    for g in range(2):
        for q, lanes, value in spread_out(z, slice(g * 256, (g + 1) * 256), spread):
            for s in range(2):
                held[4 * g + q, s, :128, lanes] = value[s * 128 : (s + 1) * 128]
        for q in range(4):
            for s in range(2):
                send(4 * g + q, s, PANEL)
    for copy in copies:
        copy.wait()


def unpack_inner_kernel(z, spread, begun, out, held, edge, sems):
    del begun
    copies = []

    def send(src, dst):
        copies.append(pltpu.make_async_copy(src, dst, sems.at[len(copies)]))
        copies[-1].start()

    for q, lanes, value in spread_out(z, slice(768, 1024), spread):
        low, high = INNER_QUARTERS[q]
        held[8, low:high, lanes] = value[96 : 96 + high - low]
        if q < 2:
            edge[q, :, lanes] = value[208:224]
        for g in range(2):
            for s in range(3):
                begin = g * 48 + s * 16
                held[4 * g + q, s * PANEL + 128 : (s + 1) * PANEL, lanes] = value[
                    begin : begin + 16
                ]
    send(held.at[8], out.at[8, PANEL : 4 * PANEL])
    for s in range(2):
        row = s * 4 * PANEL + 128
        send(edge.at[s], out.at[8, row : row + 16])
    for g in range(2):
        for q, lanes, value in spread_out(z, slice(g * 384, (g + 1) * 384), spread):
            for s in range(3):
                held[4 * g + q, s * PANEL : s * PANEL + 128, lanes] = value[
                    s * 128 : (s + 1) * 128
                ]
        for q in range(4):
            send(held.at[4 * g + q], out.at[4 * g + q, PANEL : 4 * PANEL])
    for copy in copies:
        copy.wait()


def spread_matrix():
    w, q, j = np.meshgrid(np.arange(32), np.arange(4), np.arange(4), indexing="ij")
    table = np.zeros((512, 512), np.float32)
    table[np.arange(512), (q * 128 + w * 4 + j).reshape(-1)] = 1.0
    return table


def shift_perm(count, step):
    return [(i, (i - step) % count) for i in range(count)]


def ring_gather(top, bottom):
    def up(value):
        return lax.ppermute(value, "narrow", shift_perm(NARROW, 1))

    def down(value):
        return lax.ppermute(value, "narrow", shift_perm(NARROW, -1))

    after_top, before_bottom = up(top), down(bottom)
    after_bottom, before_top = up(bottom), down(top)
    return [
        top, bottom, after_top, after_bottom,
        up(after_top), down(before_bottom), before_top, before_bottom,
    ]


def direct_gather(own):
    return [own] + [lax.ppermute(own, "narrow", shift_perm(NARROW, step)) for step in (1, 2, 3)]


def exchange(packed, chunk):
    parts = packed.reshape(WIDE, 16, chunk)
    got = lax.all_to_all(parts, "wide", split_axis=0, concat_axis=0, tiled=True)
    return got.reshape(1024, chunk)


def shards(xblk, link, order):
    rows_total = link.shape[0]
    x = jnp.transpose(xblk, (0, 2, 1, 3))
    slab = (1, ORB, PANEL, ROWS * ATOMS)
    top, bottom = pl.pallas_call(
        prep_outer_kernel,
        out_shape=[sds((SPLIT, 2944), BF16), sds((PANEL - SPLIT, 2944), BF16)],
        grid=(1,),
        in_specs=[
            SM,
            pl.BlockSpec(slab, lambda i: (0, 0, 0, 0)),
            pl.BlockSpec(slab, lambda i: (2, 0, 0, 0)),
        ],
        out_specs=[
            pl.BlockSpec((SPLIT, 2944), lambda i: (0, 0)),
            pl.BlockSpec((PANEL - SPLIT, 2944), lambda i: (0, 0)),
        ],
        compiler_params=params(48),
        name="prep_outer",
    )(link, x, x)
    gas = ring_gather(top, bottom)
    gb, a_first, a_mid, a_last, traces = pl.pallas_call(
        prep_inner_kernel,
        out_shape=[
            sds((PANEL, 2304), BF16),
            sds((3, PANEL, LANES), BF16),
            sds((2, 3, PANEL, LANES), BF16),
            sds((3, PANEL, LANES), BF16),
            sds((WIDE, 1, 128), F32),
        ],
        in_specs=[SM, VM, ANY],
        out_specs=[VM] * 5,
        compiler_params=params(48),
        name="prep_inner",
    )(link, x, top)
    a_prev = lax.ppermute(a_last, "wide", shift_perm(WIDE, -1))
    a_next = lax.ppermute(a_first, "wide", shift_perm(WIDE, 1))
    line = lax.all_to_all(traces, "wide", split_axis=0, concat_axis=0, tiled=True)
    line = jnp.sum(line, axis=0)
    sums = direct_gather(line)
    wanted = jnp.broadcast_to(order.reshape(64, 1, 4), (64, 4, 4))
    quarter = jnp.arange(4, dtype=jnp.int32).reshape(1, 4, 1)
    wanted = ((wanted // ATOMS) * 256 + quarter * ATOMS + wanted % ATOMS).reshape(1024, 1)
    quad = pl.pallas_call(
        deal_kernel,
        out_shape=sds((1024, 1024), BF16),
        in_specs=[VM],
        out_specs=VM,
        compiler_params=params(8),
        name="deal",
    )(wanted)
    gb, quad, a_prev, a_next, gas = lax.optimization_barrier((gb, quad, a_prev, a_next, gas))
    gbs = direct_gather(gb)
    lefts = (a_prev, a_first, a_mid, a_last, a_next)
    packed_outer, left_over = pl.pallas_call(
        lambda *refs: outer_kernel(rows_total, *refs),
        out_shape=[sds((1024, OUTER_CHUNK), BF16), sds((16, 1024), BF16)],
        in_specs=[VM] * 18,
        out_specs=[VM, VM],
        scratch_shapes=[
            pltpu.VMEM((ROWS + 1, ORB, NARROW, 16, LANES), BF16),
            pltpu.VMEM((OUTER_CHUNK, 1024), BF16),
        ],
        compiler_params=params(24),
        cost_estimate=pl.CostEstimate(
            flops=OUTER_FLOPS, bytes_accessed=8 << 20, transcendentals=0
        ),
        name="outer",
    )(*sums, *gas, *lefts, quad)
    got_outer = exchange(packed_outer, OUTER_CHUNK)
    packed_inner = pl.pallas_call(
        lambda *refs: inner_kernel(rows_total, *refs),
        out_shape=sds((1024, INNER_CHUNK), BF16),
        in_specs=[VM] * 23,
        out_specs=VM,
        scratch_shapes=[
            pltpu.VMEM((2 * ROWS + 1, ORB, NARROW, 16, LANES), BF16),
            pltpu.VMEM((3, PANEL, LANES), F32),
            pltpu.VMEM((INNER_CHUNK, 1024), BF16),
        ],
        compiler_params=params(54),
        cost_estimate=pl.CostEstimate(
            flops=INNER_FLOPS, bytes_accessed=12 << 20, transcendentals=0
        ),
        name="inner",
    )(*sums, *gas, *gbs, *lefts, quad, left_over)
    packed_inner, got_outer = lax.optimization_barrier((packed_inner, got_outer))
    got_inner = exchange(packed_inner, INNER_CHUNK)
    spread = jnp.asarray(spread_matrix(), BF16)
    out = pl.pallas_call(
        unpack_outer_kernel,
        out_shape=sds((ORB, 5 * PANEL, 256), BF16),
        in_specs=[VM, VM],
        out_specs=ANY,
        scratch_shapes=[
            pltpu.VMEM((ORB, 2, PANEL, 256), BF16),
            pltpu.SemaphoreType.DMA((18,)),
        ],
        compiler_params=params(14),
        name="unpack_outer",
    )(got_outer, spread)
    out = pl.pallas_call(
        unpack_inner_kernel,
        out_shape=sds((ORB, 5 * PANEL, 256), BF16),
        in_specs=[VM, VM, ANY],
        out_specs=ANY,
        scratch_shapes=[
            pltpu.VMEM((ORB, 3 * PANEL, 256), BF16),
            pltpu.VMEM((2, 16, 256), BF16),
            pltpu.SemaphoreType.DMA((11,)),
        ],
        input_output_aliases={2: 0},
        compiler_params=params(16),
        name="unpack_inner",
    )(got_inner, spread, out)
    return out.reshape(ORB, 5, PANEL, 256)


def solution(mesh):
    return jax.shard_map(
        shards,
        mesh=mesh,
        in_specs=(P(None, "narrow", None, "wide"), P(), P("wide")),
        out_specs=P(None, None, "narrow", "wide"),
        check_vma=False,
    )
```

```python
import jax
import jax.numpy as jnp
from jax import lax
from jax.experimental import pallas as pl
from jax.experimental.pallas import tpu as pltpu
from jax.sharding import PartitionSpec as P

ORB = 9
ATOMS = 64
BLOCK = 576
PANEL = 144
LANES = 640
ROWS = 4
NARROW = 4
WIDE = 64
MAIN = 512
OUTER_CHUNK = 640
INNER_CHUNK = 1024
INNER_QUARTERS = ((0, 112), (112, 224), (224, 336), (336, 432))
F32 = jnp.float32
BF16 = jnp.bfloat16
OUTER_FLOPS = 30 * 10**9
INNER_FLOPS = 70 * 10**9

VM = pl.BlockSpec(memory_space=pltpu.VMEM)
SM = pl.BlockSpec(memory_space=pltpu.SMEM)
ANY = pl.BlockSpec(memory_space=pl.ANY)
HBM = pl.BlockSpec(memory_space=pltpu.HBM)
sds = jax.ShapeDtypeStruct


def params(mib):
    return pltpu.CompilerParams(vmem_limit_bytes=mib << 20)


def lane_mask(link, first, shift):
    lanes = lax.broadcasted_iota(jnp.int32, (1, ROWS * ATOMS), 1) // ATOMS
    total = link.shape[0]
    mask = jnp.zeros((1, ROWS * ATOMS), F32)
    for r in range(ROWS):
        value = link[lax.rem(first + (r + shift + total), total)].astype(F32)
        mask = jnp.where(lanes == r, value, mask)
    return mask


def reorder_matrix():
    i = lax.broadcasted_iota(jnp.int32, (PANEL, PANEL), 0)
    c = lax.broadcasted_iota(jnp.int32, (PANEL, PANEL), 1)
    return jnp.where(c == (i % 16) * ORB + i // 16, 1.0, 0.0).astype(BF16)


def packed_row(tiles, r, pad):
    parts = [t[:, r * ATOMS : (r + 1) * ATOMS] for t in tiles]
    if pad:
        parts.append(jnp.zeros((PANEL, ATOMS), BF16))
    return jnp.concatenate(parts, axis=1)


def put_panel(out, count, p, value):
    out[:, p * MAIN : (p + 1) * MAIN] = value[:, :MAIN]
    tail = count * MAIN + p * ATOMS
    out[:, tail : tail + ATOMS] = value[:, MAIN:BLOCK]


def prep_outer_kernel(link, low, high, ga):
    first = lax.axis_index("wide") * ROWS
    before = lane_mask(link, first, -1).astype(BF16)
    after = lane_mask(link, first, 0).astype(BF16)
    reorder = reorder_matrix()
    tiles = [low[0, o] * before for o in range(ORB)]
    for p in range(ROWS + 1):
        if p == ROWS:
            tiles = [high[0, o] * after for o in range(ORB)]
        value = packed_row(tiles, min(p, ROWS - 1), False)
        turned = jnp.dot(reorder, value, preferred_element_type=F32).astype(BF16)
        put_panel(ga, ROWS + 1, p, turned)
    ga[:, (ROWS + 1) * BLOCK :] = jnp.zeros((PANEL, ATOMS), BF16)


def prep_inner_kernel(link, x, ga, gb, a_first, a_mid, a_last, traces):
    del ga
    first = lax.axis_index("wide") * ROWS
    masks = (lane_mask(link, first, -1), None, lane_mask(link, first, 0))
    squares = jnp.zeros((PANEL, ROWS * ATOMS), F32)
    for j in range(3):
        total = jnp.zeros((PANEL, ROWS * ATOMS), F32)
        for o in range(ORB):
            t = x[j, o].astype(F32)
            total = total + t * t
        if masks[j] is not None:
            total = total * masks[j]
        squares = squares + total
    narrow = lax.axis_index("narrow")
    rows = lax.broadcasted_iota(jnp.int32, (PANEL, ROWS * ATOMS), 0) + narrow * PANEL
    lanes = lax.broadcasted_iota(jnp.int32, (PANEL, ROWS * ATOMS), 1) % ATOMS
    diagonal = jnp.zeros((PANEL, ROWS * ATOMS), F32)
    for o in range(ORB):
        diagonal = diagonal + jnp.where(rows == lanes * ORB + o, x[1, o].astype(F32), 0.0)
    sq = jnp.sum(squares, axis=0, keepdims=True)
    tx = jnp.sum(diagonal, axis=0, keepdims=True)
    sq = jnp.sum(sq, axis=1, keepdims=True)
    tx = jnp.sum(tx, axis=1, keepdims=True)
    lane = lax.broadcasted_iota(jnp.int32, (1, 128), 1)
    value = jnp.where(lane == 0, tx, jnp.where(lane == 1, sq, 0.0))
    traces[...] = jnp.broadcast_to(value.reshape(1, 1, 128), (WIDE, 1, 128))
    reorder = reorder_matrix()
    for j in range(3):
        tiles = [x[j, o] for o in range(ORB)]
        if masks[j] is not None:
            tiles = [t * masks[j].astype(BF16) for t in tiles]
        for r in range(ROWS):
            value = packed_row(tiles, r, True)
            if r == 0:
                a_first[j] = value
            elif r == ROWS - 1:
                a_last[j] = value
            else:
                a_mid[r - 1, j] = value
            if j == 1:
                turned = jnp.dot(reorder, value, preferred_element_type=F32).astype(BF16)
                put_panel(gb, ROWS, r, turned)


def deal_kernel(wanted, quad):
    step = 128
    for k in range(0, 1024, step):
        lanes = lax.broadcasted_iota(jnp.int32, (step, 1024), 1)
        quad[k : k + step, :] = jnp.where(lanes == wanted[k : k + step, :], 1.0, 0.0).astype(BF16)


def nt(a, b):
    return lax.dot_general(a, b, (((1,), (1,)), ((), ())), preferred_element_type=F32)


def tn(a, b):
    return lax.dot_general(a, b, (((0,), (0,)), ((), ())), preferred_element_type=F32)


def twice_weight(sums, rows_total):
    total = sums[0][...] + sums[1][...] + sums[2][...] + sums[3][...]
    tx = total[:, 0:1]
    sq = total[:, 1:2]
    return 2.0 * jax.nn.sigmoid(4.0 * (tx - sq) / (rows_total * BLOCK) + 5.0)


def assemble(full, base, count, sources):
    narrow = lax.axis_index("narrow")
    if len(sources) == NARROW:
        places = tuple((shift, 0, ORB) for shift in range(NARROW))
    else:
        places = ((0, 0, ORB), (1, 0, ORB), (2, 0, 5), (2, 5, 4), (3, 0, ORB))
    for (shift, o, depth), src in zip(places, sources):
        owner = lax.rem(narrow + shift, NARROW)
        for p in range(count):
            value = src[:, p * MAIN : (p + 1) * MAIN]
            full[base + p, o : o + depth, pl.ds(owner, 1), :, :MAIN] = value.reshape(
                depth, 1, 16, MAIN
            )
            tail = count * MAIN + p * ATOMS
            value = src[:, tail : tail + ATOMS]
            full[base + p, o : o + depth, pl.ds(owner, 1), :, MAIN:BLOCK] = value.reshape(
                depth, 1, 16, ATOMS
            )


def put_fresh(rows, value, r, s, slabs):
    for g in range(2):
        piece = value[:, g * 256 : (g + 1) * 256].astype(BF16)
        lanes = slice(r * 256, (r + 1) * 256)
        begin = (g * slabs + s) * 128
        rows[begin : begin + 128, lanes] = piece[:128]
        begin = slabs * 256 + (g * slabs + s) * 16
        rows[begin : begin + 16, lanes] = piece[128:]


def outer_kernel(
    rows_total, sum0, sum1, sum2, sum3, ga0, ga1, ga2, ga3, ga4,
    a_prev, a_first, a_mid, a_last, a_next, quad,
    out, left_over, full, rows, held, sems,
):
    gas = (ga0, ga1, ga2, ga3, ga4)
    twice = twice_weight((sum0, sum1, sum2, sum3), rows_total)
    assemble(full, 0, ROWS + 1, gas)
    lefts = [a_prev, a_first, a_mid.at[0], a_mid.at[1], a_last, a_next]
    left_over[...] = jnp.zeros_like(left_over)
    for r in range(ROWS):
        for s in range(2):
            if s == 0:
                b = full[r].reshape(BLOCK, LANES)
                prod = jnp.dot(lefts[r][0][:, :BLOCK], b, preferred_element_type=F32)
            elif r < ROWS - 1:
                b = full[r + 1].reshape(BLOCK, LANES)[:, :BLOCK]
                prod = nt(lefts[r + 2][2][:, :BLOCK], b)
            else:
                b = full[ROWS].reshape(BLOCK, LANES)
                prod = jnp.dot(lefts[r + 2][2][:, :BLOCK], b, preferred_element_type=F32)
            value = prod + twice * (0.0 - prod)
            put_fresh(rows, value, r, s, 2)
            tail = value[:, MAIN:BLOCK].astype(BF16)
            for half in range(2):
                lane = r * 256 + (2 * s + half) * ATOMS
                rows[576:640, lane : lane + ATOMS] = tail[half * 64 : half * 64 + 64]
            lane = r * 256 + s * ATOMS
            left_over[:, lane : lane + ATOMS] = tail[128:]
    copies = []
    for k in range(0, 1024, 256):
        held[k : k + 256, :] = nt(quad[k : k + 256, :], rows[...]).astype(BF16)
        copies.append(
            pltpu.make_async_copy(
                held.at[k : k + 256], out.at[k : k + 256], sems.at[len(copies)]
            )
        )
        copies[-1].start()
    for copy in copies:
        copy.wait()


def inner_kernel(
    rows_total, sum0, sum1, sum2, sum3, ga0, ga1, ga2, ga3, ga4, gb0, gb1, gb2, gb3,
    a_prev, a_first, a_mid, a_last, a_next, quad, left_over,
    out, full, acc, rows,
):
    gas = (ga0, ga1, ga2, ga3, ga4)
    gbs = (gb0, gb1, gb2, gb3)
    twice = twice_weight((sum0, sum1, sum2, sum3), rows_total)
    assemble(full, 0, ROWS + 1, gas)
    assemble(full, ROWS + 1, ROWS, gbs)
    lefts = [a_prev, a_first, a_mid.at[0], a_mid.at[1], a_last, a_next]

    def left(r, low, high):
        return jnp.concatenate([lefts[r + 1][j][:, :BLOCK] for j in range(low, high)], axis=0)

    rows[960:976, :] = jnp.zeros((16, 1024), BF16)
    rows[976:992, :] = left_over[...]
    rows[992:, :] = jnp.zeros((32, 1024), BF16)
    for r in range(ROWS):
        value = jnp.dot(
            left(r, 0, 3), full[ROWS + 1 + r].reshape(BLOCK, LANES), preferred_element_type=F32
        )
        for s in range(3):
            acc[s] = value[s * PANEL : (s + 1) * PANEL]
        value = jnp.dot(
            left(r - 1, 1, 3), full[r].reshape(BLOCK, LANES), preferred_element_type=F32
        )
        for s in range(2):
            acc[s] += value[s * PANEL : (s + 1) * PANEL]
        if r < ROWS - 1:
            value = nt(left(r + 1, 0, 2), full[r + 1].reshape(BLOCK, LANES)[:, :BLOCK])
        else:
            value = jnp.dot(
                left(r + 1, 0, 2), full[ROWS].reshape(BLOCK, LANES), preferred_element_type=F32
            )[:, :BLOCK]
        for s in range(2):
            acc[s + 1, :, :BLOCK] += value[s * PANEL : (s + 1) * PANEL]
        for s in range(3):
            prod = acc[s]
            value = prod + twice * (lefts[r + 1][s].astype(F32) - prod)
            put_fresh(rows, value, r, s, 3)
            tail = value[:, MAIN:BLOCK].astype(BF16)
            for q, (low, high) in enumerate(INNER_QUARTERS):
                begin, end = max(low, s * PANEL), min(high, (s + 1) * PANEL)
                if begin < end:
                    lane = r * 256 + q * ATOMS
                    rows[864 + begin - low : 864 + end - low, lane : lane + ATOMS] = tail[
                        begin - s * PANEL : end - s * PANEL
                    ]
    for k in range(0, 1024, 256):
        out[k : k + 256, :] = nt(quad[k : k + 256, :], rows[...]).astype(BF16)


def spread_matrix():
    i = lax.broadcasted_iota(jnp.int32, (512, 512), 0)
    lane = lax.broadcasted_iota(jnp.int32, (512, 512), 1)
    wanted = ((i // 4) % 4) * 128 + (i // 16) * 4 + i % 4
    return jnp.where(lane == wanted, 1.0, 0.0).astype(BF16)


def spread_out(z, lanes, spread):
    for half in range(2):
        value = tn(z[half * 512 : (half + 1) * 512, lanes], spread[...]).astype(BF16)
        for q in range(4):
            yield q, slice(half * 128, (half + 1) * 128), value[:, q * 128 : (q + 1) * 128]


def unpack_outer_kernel(z, out, spread, held, sems):
    spread[...] = spread_matrix()
    copies = []

    def send(o, s, high):
        row = s * 4 * PANEL
        copies.append(
            pltpu.make_async_copy(
                held.at[o, s, :high], out.at[o, row : row + high], sems.at[len(copies)]
            )
        )
        copies[-1].start()

    for q, lanes, value in spread_out(z, slice(512, 640), spread):
        held[8, q // 2, (q % 2) * 64 : (q % 2) * 64 + 64, lanes] = value[64:]
        for g in range(2):
            for s in range(2):
                begin = g * 32 + s * 16
                held[4 * g + q, s, 128:, lanes] = value[begin : begin + 16]
    for s in range(2):
        send(8, s, 128)
    for g in range(2):
        for q, lanes, value in spread_out(z, slice(g * 256, (g + 1) * 256), spread):
            for s in range(2):
                held[4 * g + q, s, :128, lanes] = value[s * 128 : (s + 1) * 128]
        for q in range(4):
            for s in range(2):
                send(4 * g + q, s, PANEL)
    for copy in copies:
        copy.wait()


def unpack_inner_kernel(z, begun, out, spread, held, edge, sems):
    del begun
    spread[...] = spread_matrix()
    copies = []

    def send(src, dst):
        copies.append(pltpu.make_async_copy(src, dst, sems.at[len(copies)]))
        copies[-1].start()

    for q, lanes, value in spread_out(z, slice(768, 1024), spread):
        low, high = INNER_QUARTERS[q]
        held[8, low:high, lanes] = value[96 : 96 + high - low]
        if q < 2:
            edge[q, :, lanes] = value[208:224]
        for g in range(2):
            for s in range(3):
                begin = g * 48 + s * 16
                held[4 * g + q, s * PANEL + 128 : (s + 1) * PANEL, lanes] = value[
                    begin : begin + 16
                ]
    send(held.at[8], out.at[8, PANEL : 4 * PANEL])
    for s in range(2):
        row = s * 4 * PANEL + 128
        send(edge.at[s], out.at[8, row : row + 16])
    for g in range(2):
        for q, lanes, value in spread_out(z, slice(g * 384, (g + 1) * 384), spread):
            for s in range(3):
                held[4 * g + q, s * PANEL : s * PANEL + 128, lanes] = value[
                    s * 128 : (s + 1) * 128
                ]
        for q in range(4):
            send(held.at[4 * g + q], out.at[4 * g + q, PANEL : 4 * PANEL])
    for copy in copies:
        copy.wait()


def shift_perm(count, step):
    return [(i, (i - step) % count) for i in range(count)]


def neighbours(own):
    after = lax.ppermute(own, "narrow", shift_perm(NARROW, 1))
    before = lax.ppermute(own, "narrow", shift_perm(NARROW, -1))
    return after, before


def opposite(after, before):
    split = 80
    top, bottom = lax.optimization_barrier((after[:split], before[split:]))
    top = lax.ppermute(top, "narrow", shift_perm(NARROW, 1))
    bottom = lax.ppermute(bottom, "narrow", shift_perm(NARROW, -1))
    return top, bottom


def direct_gather(own):
    return [own] + [lax.ppermute(own, "narrow", shift_perm(NARROW, step)) for step in (1, 2, 3)]


def exchange(packed, chunk):
    parts = packed.reshape(WIDE, 16, chunk)
    got = lax.all_to_all(parts, "wide", split_axis=0, concat_axis=0, tiled=True)
    return got.reshape(1024, chunk)


def shards(xblk, link, order):
    rows_total = link.shape[0]
    x = jnp.transpose(xblk, (0, 2, 1, 3))
    slab = (1, ORB, PANEL, ROWS * ATOMS)
    ga = pl.pallas_call(
        prep_outer_kernel,
        out_shape=sds((PANEL, 2944), BF16),
        grid=(1,),
        in_specs=[
            SM,
            pl.BlockSpec(slab, lambda i: (0, 0, 0, 0)),
            pl.BlockSpec(slab, lambda i: (2, 0, 0, 0)),
        ],
        out_specs=pl.BlockSpec((PANEL, 2944), lambda i: (0, 0)),
        compiler_params=params(48),
        name="prep_outer",
    )(link, x, x)
    after, before = neighbours(ga)
    gb, a_first, a_mid, a_last, traces = pl.pallas_call(
        prep_inner_kernel,
        out_shape=[
            sds((PANEL, 2304), BF16),
            sds((3, PANEL, LANES), BF16),
            sds((2, 3, PANEL, LANES), BF16),
            sds((3, PANEL, LANES), BF16),
            sds((WIDE, 1, 128), F32),
        ],
        in_specs=[SM, VM, ANY],
        out_specs=[VM] * 5,
        compiler_params=params(48),
        name="prep_inner",
    )(link, x, ga)
    a_prev = lax.ppermute(a_last, "wide", shift_perm(WIDE, -1))
    a_next = lax.ppermute(a_first, "wide", shift_perm(WIDE, 1))
    line = lax.all_to_all(traces, "wide", split_axis=0, concat_axis=0, tiled=True)
    line = jnp.sum(line, axis=0)
    sums = direct_gather(line)
    after, before, a_prev, a_next = lax.optimization_barrier((after, before, a_prev, a_next))
    gas = (ga, after, *opposite(after, before), before)
    wanted = jnp.broadcast_to(order.reshape(64, 1, 4), (64, 4, 4))
    quarter = jnp.arange(4, dtype=jnp.int32).reshape(1, 4, 1)
    wanted = ((wanted // ATOMS) * 256 + quarter * ATOMS + wanted % ATOMS).reshape(1024, 1)
    quad = pl.pallas_call(
        deal_kernel,
        out_shape=sds((1024, 1024), BF16),
        in_specs=[VM],
        out_specs=VM,
        compiler_params=params(8),
        name="deal",
    )(wanted)
    gb, quad, a_prev, a_next = lax.optimization_barrier((gb, quad, a_prev, a_next))
    gbs = direct_gather(gb)
    lefts = (a_prev, a_first, a_mid, a_last, a_next)
    packed_outer, left_over = pl.pallas_call(
        lambda *refs: outer_kernel(rows_total, *refs),
        out_shape=[sds((1024, OUTER_CHUNK), BF16), sds((16, 1024), BF16)],
        in_specs=[VM] * 15,
        out_specs=[HBM, VM],
        scratch_shapes=[
            pltpu.VMEM((ROWS + 1, ORB, NARROW, 16, LANES), BF16),
            pltpu.VMEM((OUTER_CHUNK, 1024), BF16),
            pltpu.VMEM((1024, OUTER_CHUNK), BF16),
            pltpu.SemaphoreType.DMA((4,)),
        ],
        compiler_params=params(24),
        cost_estimate=pl.CostEstimate(
            flops=OUTER_FLOPS, bytes_accessed=8 << 20, transcendentals=0
        ),
        name="outer",
    )(*sums, *gas, *lefts, quad)
    got_outer = exchange(packed_outer, OUTER_CHUNK)
    packed_inner = pl.pallas_call(
        lambda *refs: inner_kernel(rows_total, *refs),
        out_shape=sds((1024, INNER_CHUNK), BF16),
        in_specs=[VM] * 20,
        out_specs=VM,
        scratch_shapes=[
            pltpu.VMEM((2 * ROWS + 1, ORB, NARROW, 16, LANES), BF16),
            pltpu.VMEM((3, PANEL, LANES), F32),
            pltpu.VMEM((INNER_CHUNK, 1024), BF16),
        ],
        compiler_params=params(54),
        cost_estimate=pl.CostEstimate(
            flops=INNER_FLOPS, bytes_accessed=12 << 20, transcendentals=0
        ),
        name="inner",
    )(*sums, *gas, *gbs, *lefts, quad, left_over)
    packed_inner, got_outer = lax.optimization_barrier((packed_inner, got_outer))
    got_inner = exchange(packed_inner, INNER_CHUNK)
    out = pl.pallas_call(
        unpack_outer_kernel,
        out_shape=sds((ORB, 5 * PANEL, 256), BF16),
        in_specs=[VM],
        out_specs=ANY,
        scratch_shapes=[
            pltpu.VMEM((512, 512), BF16),
            pltpu.VMEM((ORB, 2, PANEL, 256), BF16),
            pltpu.SemaphoreType.DMA((18,)),
        ],
        compiler_params=params(14),
        name="unpack_outer",
    )(got_outer)
    out = pl.pallas_call(
        unpack_inner_kernel,
        out_shape=sds((ORB, 5 * PANEL, 256), BF16),
        in_specs=[VM, ANY],
        out_specs=ANY,
        scratch_shapes=[
            pltpu.VMEM((512, 512), BF16),
            pltpu.VMEM((ORB, 3 * PANEL, 256), BF16),
            pltpu.VMEM((2, 16, 256), BF16),
            pltpu.SemaphoreType.DMA((11,)),
        ],
        input_output_aliases={1: 0},
        compiler_params=params(16),
        name="unpack_inner",
    )(got_inner, out)
    return out.reshape(ORB, 5, PANEL, 256)


def solution(mesh):
    return jax.shard_map(
        shards,
        mesh=mesh,
        in_specs=(P(None, "narrow", None, "wide"), P(), P("wide")),
        out_specs=P(None, None, "narrow", "wide"),
        check_vma=False,
    )
```

```python
import jax
import jax.numpy as jnp
from jax import lax
from jax.experimental import pallas as pl
from jax.experimental.pallas import tpu as pltpu
from jax.sharding import PartitionSpec as P

ORB = 9
ATOMS = 64
BLOCK = 576
PANEL = 144
LANES = 640
ROWS = 4
NARROW = 4
WIDE = 64
MAIN = 512
OUTER_CHUNK = 640
INNER_CHUNK = 1024
INNER_QUARTERS = ((0, 112), (112, 224), (224, 336), (336, 432))
F32 = jnp.float32
BF16 = jnp.bfloat16
OUTER_FLOPS = 30 * 10**9
INNER_FLOPS = 70 * 10**9

VM = pl.BlockSpec(memory_space=pltpu.VMEM)
SM = pl.BlockSpec(memory_space=pltpu.SMEM)
ANY = pl.BlockSpec(memory_space=pl.ANY)
HBM = pl.BlockSpec(memory_space=pltpu.HBM)
sds = jax.ShapeDtypeStruct


def params(mib):
    return pltpu.CompilerParams(vmem_limit_bytes=mib << 20)


def lane_mask(link, first, shift):
    lanes = lax.broadcasted_iota(jnp.int32, (1, ROWS * ATOMS), 1) // ATOMS
    total = link.shape[0]
    mask = jnp.zeros((1, ROWS * ATOMS), F32)
    for r in range(ROWS):
        value = link[lax.rem(first + (r + shift + total), total)].astype(F32)
        mask = jnp.where(lanes == r, value, mask)
    return mask


def reorder_matrix():
    i = lax.broadcasted_iota(jnp.int32, (PANEL, PANEL), 0)
    c = lax.broadcasted_iota(jnp.int32, (PANEL, PANEL), 1)
    return jnp.where(c == (i % 16) * ORB + i // 16, 1.0, 0.0).astype(BF16)


def packed_row(tiles, r, pad):
    parts = [t[:, r * ATOMS : (r + 1) * ATOMS] for t in tiles]
    if pad:
        parts.append(jnp.zeros((PANEL, ATOMS), BF16))
    return jnp.concatenate(parts, axis=1)


def put_panel(out, count, p, value):
    out[:, p * MAIN : (p + 1) * MAIN] = value[:, :MAIN]
    tail = count * MAIN + p * ATOMS
    out[:, tail : tail + ATOMS] = value[:, MAIN:BLOCK]


def prep_outer_kernel(link, low, high, ga):
    first = lax.axis_index("wide") * ROWS
    before = lane_mask(link, first, -1).astype(BF16)
    after = lane_mask(link, first, 0).astype(BF16)
    reorder = reorder_matrix()
    tiles = [low[0, o] * before for o in range(ORB)]
    for p in range(ROWS + 1):
        if p == ROWS:
            tiles = [high[0, o] * after for o in range(ORB)]
        value = packed_row(tiles, min(p, ROWS - 1), False)
        turned = jnp.dot(reorder, value, preferred_element_type=F32).astype(BF16)
        put_panel(ga, ROWS + 1, p, turned)
    ga[:, (ROWS + 1) * BLOCK :] = jnp.zeros((PANEL, ATOMS), BF16)


def prep_inner_kernel(link, x, ga, gb, a_first, a_mid, a_last, traces):
    del ga
    first = lax.axis_index("wide") * ROWS
    masks = (lane_mask(link, first, -1), None, lane_mask(link, first, 0))
    squares = jnp.zeros((PANEL, ROWS * ATOMS), F32)
    for j in range(3):
        total = jnp.zeros((PANEL, ROWS * ATOMS), F32)
        for o in range(ORB):
            t = x[j, o].astype(F32)
            total = total + t * t
        if masks[j] is not None:
            total = total * masks[j]
        squares = squares + total
    narrow = lax.axis_index("narrow")
    rows = lax.broadcasted_iota(jnp.int32, (PANEL, ROWS * ATOMS), 0) + narrow * PANEL
    lanes = lax.broadcasted_iota(jnp.int32, (PANEL, ROWS * ATOMS), 1) % ATOMS
    diagonal = jnp.zeros((PANEL, ROWS * ATOMS), F32)
    for o in range(ORB):
        diagonal = diagonal + jnp.where(rows == lanes * ORB + o, x[1, o].astype(F32), 0.0)
    sq = jnp.sum(squares, axis=0, keepdims=True)
    tx = jnp.sum(diagonal, axis=0, keepdims=True)
    sq = jnp.sum(sq, axis=1, keepdims=True)
    tx = jnp.sum(tx, axis=1, keepdims=True)
    lane = lax.broadcasted_iota(jnp.int32, (1, 128), 1)
    value = jnp.where(lane == 0, tx, jnp.where(lane == 1, sq, 0.0))
    traces[...] = jnp.broadcast_to(value.reshape(1, 1, 128), (WIDE, 1, 128))
    reorder = reorder_matrix()
    for j in range(3):
        tiles = [x[j, o] for o in range(ORB)]
        if masks[j] is not None:
            tiles = [t * masks[j].astype(BF16) for t in tiles]
        for r in range(ROWS):
            value = packed_row(tiles, r, True)
            if r == 0:
                a_first[j] = value
            elif r == ROWS - 1:
                a_last[j] = value
            else:
                a_mid[r - 1, j] = value
            if j == 1:
                turned = jnp.dot(reorder, value, preferred_element_type=F32).astype(BF16)
                put_panel(gb, ROWS, r, turned)


def deal_kernel(wanted, quad):
    step = 128
    for k in range(0, 1024, step):
        lanes = lax.broadcasted_iota(jnp.int32, (step, 1024), 1)
        quad[k : k + step, :] = jnp.where(lanes == wanted[k : k + step, :], 1.0, 0.0).astype(BF16)


def nt(a, b):
    return lax.dot_general(a, b, (((1,), (1,)), ((), ())), preferred_element_type=F32)


def tn(a, b):
    return lax.dot_general(a, b, (((0,), (0,)), ((), ())), preferred_element_type=F32)


def twice_weight(sums, rows_total):
    total = jnp.sum(sums[0][...] + sums[1][...] + sums[2][...] + sums[3][...], axis=0)
    tx = total[:, 0:1]
    sq = total[:, 1:2]
    return 2.0 * jax.nn.sigmoid(4.0 * (tx - sq) / (rows_total * BLOCK) + 5.0)


def assemble(full, base, count, sources):
    narrow = lax.axis_index("narrow")
    if len(sources) == NARROW:
        places = tuple((shift, 0, ORB) for shift in range(NARROW))
    else:
        places = ((0, 0, ORB), (1, 0, ORB), (2, 0, 5), (2, 5, 4), (3, 0, ORB))
    for (shift, o, depth), src in zip(places, sources):
        owner = lax.rem(narrow + shift, NARROW)
        for p in range(count):
            value = src[:, p * MAIN : (p + 1) * MAIN]
            full[base + p, o : o + depth, pl.ds(owner, 1), :, :MAIN] = value.reshape(
                depth, 1, 16, MAIN
            )
            tail = count * MAIN + p * ATOMS
            value = src[:, tail : tail + ATOMS]
            full[base + p, o : o + depth, pl.ds(owner, 1), :, MAIN:BLOCK] = value.reshape(
                depth, 1, 16, ATOMS
            )


def put_fresh(rows, value, r, s, slabs):
    for g in range(2):
        piece = value[:, g * 256 : (g + 1) * 256].astype(BF16)
        lanes = slice(r * 256, (r + 1) * 256)
        begin = (g * slabs + s) * 128
        rows[begin : begin + 128, lanes] = piece[:128]
        begin = slabs * 256 + (g * slabs + s) * 16
        rows[begin : begin + 16, lanes] = piece[128:]


def outer_kernel(
    rows_total, sum0, sum1, sum2, sum3, ga0, ga1, ga2, ga3, ga4,
    a_prev, a_first, a_mid, a_last, a_next, quad,
    out, left_over, full, rows, held, sems,
):
    gas = (ga0, ga1, ga2, ga3, ga4)
    twice = twice_weight((sum0, sum1, sum2, sum3), rows_total)
    assemble(full, 0, ROWS + 1, gas)
    lefts = [a_prev, a_first, a_mid.at[0], a_mid.at[1], a_last, a_next]
    left_over[...] = jnp.zeros_like(left_over)
    for r in range(ROWS):
        for s in range(2):
            if s == 0:
                b = full[r].reshape(BLOCK, LANES)
                prod = jnp.dot(lefts[r][0][:, :BLOCK], b, preferred_element_type=F32)
            elif r < ROWS - 1:
                b = full[r + 1].reshape(BLOCK, LANES)[:, :BLOCK]
                prod = nt(lefts[r + 2][2][:, :BLOCK], b)
            else:
                b = full[ROWS].reshape(BLOCK, LANES)
                prod = jnp.dot(lefts[r + 2][2][:, :BLOCK], b, preferred_element_type=F32)
            value = prod + twice * (0.0 - prod)
            put_fresh(rows, value, r, s, 2)
            tail = value[:, MAIN:BLOCK].astype(BF16)
            for half in range(2):
                lane = r * 256 + (2 * s + half) * ATOMS
                rows[576:640, lane : lane + ATOMS] = tail[half * 64 : half * 64 + 64]
            lane = r * 256 + s * ATOMS
            left_over[:, lane : lane + ATOMS] = tail[128:]
    copies = []
    for k in range(0, 1024, 256):
        held[k : k + 256, :] = nt(quad[k : k + 256, :], rows[...]).astype(BF16)
        copies.append(
            pltpu.make_async_copy(
                held.at[k : k + 256], out.at[k : k + 256], sems.at[len(copies)]
            )
        )
        copies[-1].start()
    for copy in copies:
        copy.wait()


def inner_kernel(
    rows_total, sum0, sum1, sum2, sum3, ga0, ga1, ga2, ga3, ga4, gb0, gb1, gb2, gb3,
    a_prev, a_first, a_mid, a_last, a_next, quad, left_over,
    out, full, acc, rows,
):
    gas = (ga0, ga1, ga2, ga3, ga4)
    gbs = (gb0, gb1, gb2, gb3)
    twice = twice_weight((sum0, sum1, sum2, sum3), rows_total)
    assemble(full, 0, ROWS + 1, gas)
    assemble(full, ROWS + 1, ROWS, gbs)
    lefts = [a_prev, a_first, a_mid.at[0], a_mid.at[1], a_last, a_next]

    def left(r, low, high):
        return jnp.concatenate([lefts[r + 1][j][:, :BLOCK] for j in range(low, high)], axis=0)

    rows[960:976, :] = jnp.zeros((16, 1024), BF16)
    rows[976:992, :] = left_over[...]
    rows[992:, :] = jnp.zeros((32, 1024), BF16)
    for r in range(ROWS):
        value = jnp.dot(
            left(r, 0, 3), full[ROWS + 1 + r].reshape(BLOCK, LANES), preferred_element_type=F32
        )
        for s in range(3):
            acc[s] = value[s * PANEL : (s + 1) * PANEL]
        value = jnp.dot(
            left(r - 1, 1, 3), full[r].reshape(BLOCK, LANES), preferred_element_type=F32
        )
        for s in range(2):
            acc[s] += value[s * PANEL : (s + 1) * PANEL]
        if r < ROWS - 1:
            value = nt(left(r + 1, 0, 2), full[r + 1].reshape(BLOCK, LANES)[:, :BLOCK])
        else:
            value = jnp.dot(
                left(r + 1, 0, 2), full[ROWS].reshape(BLOCK, LANES), preferred_element_type=F32
            )[:, :BLOCK]
        for s in range(2):
            acc[s + 1, :, :BLOCK] += value[s * PANEL : (s + 1) * PANEL]
        for s in range(3):
            prod = acc[s]
            value = prod + twice * (lefts[r + 1][s].astype(F32) - prod)
            put_fresh(rows, value, r, s, 3)
            tail = value[:, MAIN:BLOCK].astype(BF16)
            for q, (low, high) in enumerate(INNER_QUARTERS):
                begin, end = max(low, s * PANEL), min(high, (s + 1) * PANEL)
                if begin < end:
                    lane = r * 256 + q * ATOMS
                    rows[864 + begin - low : 864 + end - low, lane : lane + ATOMS] = tail[
                        begin - s * PANEL : end - s * PANEL
                    ]
    for k in range(0, 1024, 256):
        out[k : k + 256, :] = nt(quad[k : k + 256, :], rows[...]).astype(BF16)


def spread_matrix():
    i = lax.broadcasted_iota(jnp.int32, (512, 512), 0)
    lane = lax.broadcasted_iota(jnp.int32, (512, 512), 1)
    wanted = ((i // 4) % 4) * 128 + (i // 16) * 4 + i % 4
    return jnp.where(lane == wanted, 1.0, 0.0).astype(BF16)


def spread_out(z, lanes, spread):
    for half in range(2):
        value = tn(z[half * 512 : (half + 1) * 512, lanes], spread[...]).astype(BF16)
        for q in range(4):
            yield q, slice(half * 128, (half + 1) * 128), value[:, q * 128 : (q + 1) * 128]


def unpack_outer_kernel(z, out, spread, held, sems):
    spread[...] = spread_matrix()
    copies = []

    def send(o, s, high):
        row = s * 4 * PANEL
        copies.append(
            pltpu.make_async_copy(
                held.at[o, s, :high], out.at[o, row : row + high], sems.at[len(copies)]
            )
        )
        copies[-1].start()

    for q, lanes, value in spread_out(z, slice(512, 640), spread):
        held[8, q // 2, (q % 2) * 64 : (q % 2) * 64 + 64, lanes] = value[64:]
        for g in range(2):
            for s in range(2):
                begin = g * 32 + s * 16
                held[4 * g + q, s, 128:, lanes] = value[begin : begin + 16]
    for s in range(2):
        send(8, s, 128)
    for g in range(2):
        for q, lanes, value in spread_out(z, slice(g * 256, (g + 1) * 256), spread):
            for s in range(2):
                held[4 * g + q, s, :128, lanes] = value[s * 128 : (s + 1) * 128]
        for q in range(4):
            for s in range(2):
                send(4 * g + q, s, PANEL)
    for copy in copies:
        copy.wait()


def unpack_inner_kernel(z, begun, out, spread, held, edge, sems):
    del begun
    spread[...] = spread_matrix()
    copies = []

    def send(src, dst):
        copies.append(pltpu.make_async_copy(src, dst, sems.at[len(copies)]))
        copies[-1].start()

    for q, lanes, value in spread_out(z, slice(768, 1024), spread):
        low, high = INNER_QUARTERS[q]
        held[8, low:high, lanes] = value[96 : 96 + high - low]
        if q < 2:
            edge[q, :, lanes] = value[208:224]
        for g in range(2):
            for s in range(3):
                begin = g * 48 + s * 16
                held[4 * g + q, s * PANEL + 128 : (s + 1) * PANEL, lanes] = value[
                    begin : begin + 16
                ]
    send(held.at[8], out.at[8, PANEL : 4 * PANEL])
    for s in range(2):
        row = s * 4 * PANEL + 128
        send(edge.at[s], out.at[8, row : row + 16])
    for g in range(2):
        for q, lanes, value in spread_out(z, slice(g * 384, (g + 1) * 384), spread):
            for s in range(3):
                held[4 * g + q, s * PANEL : s * PANEL + 128, lanes] = value[
                    s * 128 : (s + 1) * 128
                ]
        for q in range(4):
            send(held.at[4 * g + q], out.at[4 * g + q, PANEL : 4 * PANEL])
    for copy in copies:
        copy.wait()


def shift_perm(count, step):
    return [(i, (i - step) % count) for i in range(count)]


def neighbours(own):
    after = lax.ppermute(own, "narrow", shift_perm(NARROW, 1))
    before = lax.ppermute(own, "narrow", shift_perm(NARROW, -1))
    return after, before


def opposite(after, before):
    split = 80
    top, bottom = lax.optimization_barrier((after[:split], before[split:]))
    top = lax.ppermute(top, "narrow", shift_perm(NARROW, 1))
    bottom = lax.ppermute(bottom, "narrow", shift_perm(NARROW, -1))
    return top, bottom


def direct_gather(own):
    return [own] + [lax.ppermute(own, "narrow", shift_perm(NARROW, step)) for step in (1, 2, 3)]


def exchange(packed, chunk):
    parts = packed.reshape(WIDE, 16, chunk)
    got = lax.all_to_all(parts, "wide", split_axis=0, concat_axis=0, tiled=True)
    return got.reshape(1024, chunk)


def shards(xblk, link, order):
    rows_total = link.shape[0]
    x = jnp.transpose(xblk, (0, 2, 1, 3))
    slab = (1, ORB, PANEL, ROWS * ATOMS)
    ga = pl.pallas_call(
        prep_outer_kernel,
        out_shape=sds((PANEL, 2944), BF16),
        grid=(1,),
        in_specs=[
            SM,
            pl.BlockSpec(slab, lambda i: (0, 0, 0, 0)),
            pl.BlockSpec(slab, lambda i: (2, 0, 0, 0)),
        ],
        out_specs=pl.BlockSpec((PANEL, 2944), lambda i: (0, 0)),
        compiler_params=params(48),
        name="prep_outer",
    )(link, x, x)
    after, before = neighbours(ga)
    gb, a_first, a_mid, a_last, traces = pl.pallas_call(
        prep_inner_kernel,
        out_shape=[
            sds((PANEL, 2304), BF16),
            sds((3, PANEL, LANES), BF16),
            sds((2, 3, PANEL, LANES), BF16),
            sds((3, PANEL, LANES), BF16),
            sds((WIDE, 1, 128), F32),
        ],
        in_specs=[SM, VM, ANY],
        out_specs=[VM] * 5,
        compiler_params=params(48),
        name="prep_inner",
    )(link, x, ga)
    a_prev = lax.ppermute(a_last, "wide", shift_perm(WIDE, -1))
    a_next = lax.ppermute(a_first, "wide", shift_perm(WIDE, 1))
    line = lax.all_to_all(traces, "wide", split_axis=0, concat_axis=0, tiled=True)
    sums = direct_gather(line)
    after, before, a_prev, a_next = lax.optimization_barrier((after, before, a_prev, a_next))
    gas = (ga, after, *opposite(after, before), before)
    wanted = jnp.broadcast_to(order.reshape(64, 1, 4), (64, 4, 4))
    quarter = jnp.arange(4, dtype=jnp.int32).reshape(1, 4, 1)
    wanted = ((wanted // ATOMS) * 256 + quarter * ATOMS + wanted % ATOMS).reshape(1024, 1)
    quad = pl.pallas_call(
        deal_kernel,
        out_shape=sds((1024, 1024), BF16),
        in_specs=[VM],
        out_specs=VM,
        compiler_params=params(8),
        name="deal",
    )(wanted)
    gb, quad, a_prev, a_next, *_ = lax.optimization_barrier((gb, quad, a_prev, a_next, sums[1]))
    gbs = direct_gather(gb)
    lefts = (a_prev, a_first, a_mid, a_last, a_next)
    packed_outer, left_over = pl.pallas_call(
        lambda *refs: outer_kernel(rows_total, *refs),
        out_shape=[sds((1024, OUTER_CHUNK), BF16), sds((16, 1024), BF16)],
        in_specs=[VM] * 15,
        out_specs=[HBM, VM],
        scratch_shapes=[
            pltpu.VMEM((ROWS + 1, ORB, NARROW, 16, LANES), BF16),
            pltpu.VMEM((OUTER_CHUNK, 1024), BF16),
            pltpu.VMEM((1024, OUTER_CHUNK), BF16),
            pltpu.SemaphoreType.DMA((4,)),
        ],
        compiler_params=params(24),
        cost_estimate=pl.CostEstimate(
            flops=OUTER_FLOPS, bytes_accessed=8 << 20, transcendentals=0
        ),
        name="outer",
    )(*sums, *gas, *lefts, quad)
    got_outer = exchange(packed_outer, OUTER_CHUNK)
    packed_inner = pl.pallas_call(
        lambda *refs: inner_kernel(rows_total, *refs),
        out_shape=sds((1024, INNER_CHUNK), BF16),
        in_specs=[VM] * 20,
        out_specs=VM,
        scratch_shapes=[
            pltpu.VMEM((2 * ROWS + 1, ORB, NARROW, 16, LANES), BF16),
            pltpu.VMEM((3, PANEL, LANES), F32),
            pltpu.VMEM((INNER_CHUNK, 1024), BF16),
        ],
        compiler_params=params(54),
        cost_estimate=pl.CostEstimate(
            flops=INNER_FLOPS, bytes_accessed=12 << 20, transcendentals=0
        ),
        name="inner",
    )(*sums, *gas, *gbs, *lefts, quad, left_over)
    packed_inner, got_outer = lax.optimization_barrier((packed_inner, got_outer))
    got_inner = exchange(packed_inner, INNER_CHUNK)
    out = pl.pallas_call(
        unpack_outer_kernel,
        out_shape=sds((ORB, 5 * PANEL, 256), BF16),
        in_specs=[VM],
        out_specs=ANY,
        scratch_shapes=[
            pltpu.VMEM((512, 512), BF16),
            pltpu.VMEM((ORB, 2, PANEL, 256), BF16),
            pltpu.SemaphoreType.DMA((18,)),
        ],
        compiler_params=params(14),
        name="unpack_outer",
    )(got_outer)
    out = pl.pallas_call(
        unpack_inner_kernel,
        out_shape=sds((ORB, 5 * PANEL, 256), BF16),
        in_specs=[VM, ANY],
        out_specs=ANY,
        scratch_shapes=[
            pltpu.VMEM((512, 512), BF16),
            pltpu.VMEM((ORB, 3 * PANEL, 256), BF16),
            pltpu.VMEM((2, 16, 256), BF16),
            pltpu.SemaphoreType.DMA((11,)),
        ],
        input_output_aliases={1: 0},
        compiler_params=params(16),
        name="unpack_inner",
    )(got_inner, out)
    return out.reshape(ORB, 5, PANEL, 256)


def solution(mesh):
    return jax.shard_map(
        shards,
        mesh=mesh,
        in_specs=(P(None, "narrow", None, "wide"), P(), P("wide")),
        out_specs=P(None, None, "narrow", "wide"),
        check_vma=False,
    )
```

```python
import jax
import jax.numpy as jnp
from jax import lax
from jax.experimental import pallas as pl
from jax.experimental.pallas import tpu as pltpu
from jax.sharding import PartitionSpec as P

ORB = 9
ATOMS = 64
BLOCK = 576
PANEL = 144
LANES = 640
ROWS = 4
NARROW = 4
WIDE = 64
MAIN = 512
OUTER_CHUNK = 640
INNER_CHUNK = 1024
INNER_QUARTERS = ((0, 112), (112, 224), (224, 336), (336, 432))
F32 = jnp.float32
BF16 = jnp.bfloat16
OUTER_FLOPS = 30 * 10**9
INNER_FLOPS = 70 * 10**9

VM = pl.BlockSpec(memory_space=pltpu.VMEM)
SM = pl.BlockSpec(memory_space=pltpu.SMEM)
ANY = pl.BlockSpec(memory_space=pl.ANY)
HBM = pl.BlockSpec(memory_space=pltpu.HBM)
sds = jax.ShapeDtypeStruct


def params(mib):
    return pltpu.CompilerParams(vmem_limit_bytes=mib << 20)


def lane_mask(link, first, shift):
    lanes = lax.broadcasted_iota(jnp.int32, (1, ROWS * ATOMS), 1) // ATOMS
    total = link.shape[0]
    mask = jnp.zeros((1, ROWS * ATOMS), F32)
    for r in range(ROWS):
        value = link[lax.rem(first + (r + shift + total), total)].astype(F32)
        mask = jnp.where(lanes == r, value, mask)
    return mask


def reorder_matrix():
    i = lax.broadcasted_iota(jnp.int32, (PANEL, PANEL), 0)
    c = lax.broadcasted_iota(jnp.int32, (PANEL, PANEL), 1)
    return jnp.where(c == (i % 16) * ORB + i // 16, 1.0, 0.0).astype(BF16)


def packed_row(tiles, r, pad):
    parts = [t[:, r * ATOMS : (r + 1) * ATOMS] for t in tiles]
    if pad:
        parts.append(jnp.zeros((PANEL, ATOMS), BF16))
    return jnp.concatenate(parts, axis=1)


def put_panel(out, count, p, value):
    out[:, p * MAIN : (p + 1) * MAIN] = value[:, :MAIN]
    tail = count * MAIN + p * ATOMS
    out[:, tail : tail + ATOMS] = value[:, MAIN:BLOCK]


def prep_outer_kernel(link, low, high, ga):
    first = lax.axis_index("wide") * ROWS
    before = lane_mask(link, first, -1).astype(BF16)
    after = lane_mask(link, first, 0).astype(BF16)
    reorder = reorder_matrix()
    tiles = [low[0, o] * before for o in range(ORB)]
    for p in range(ROWS + 1):
        if p == ROWS:
            tiles = [high[0, o] * after for o in range(ORB)]
        value = packed_row(tiles, min(p, ROWS - 1), False)
        turned = jnp.dot(reorder, value, preferred_element_type=F32).astype(BF16)
        put_panel(ga, ROWS + 1, p, turned)
    ga[:, (ROWS + 1) * BLOCK :] = jnp.zeros((PANEL, ATOMS), BF16)


def prep_inner_kernel(link, x, ga, gb, a_first, a_mid, a_last, traces):
    del ga
    first = lax.axis_index("wide") * ROWS
    masks = (lane_mask(link, first, -1), None, lane_mask(link, first, 0))
    squares = jnp.zeros((PANEL, ROWS * ATOMS), F32)
    for j in range(3):
        total = jnp.zeros((PANEL, ROWS * ATOMS), F32)
        for o in range(ORB):
            t = x[j, o].astype(F32)
            total = total + t * t
        if masks[j] is not None:
            total = total * masks[j]
        squares = squares + total
    narrow = lax.axis_index("narrow")
    rows = lax.broadcasted_iota(jnp.int32, (PANEL, ROWS * ATOMS), 0) + narrow * PANEL
    lanes = lax.broadcasted_iota(jnp.int32, (PANEL, ROWS * ATOMS), 1) % ATOMS
    diagonal = jnp.zeros((PANEL, ROWS * ATOMS), F32)
    for o in range(ORB):
        diagonal = diagonal + jnp.where(rows == lanes * ORB + o, x[1, o].astype(F32), 0.0)
    sq = jnp.sum(squares, axis=0, keepdims=True)
    tx = jnp.sum(diagonal, axis=0, keepdims=True)
    sq = jnp.sum(sq, axis=1, keepdims=True)
    tx = jnp.sum(tx, axis=1, keepdims=True)
    lane = lax.broadcasted_iota(jnp.int32, (1, 128), 1)
    value = jnp.where(lane == 0, tx, jnp.where(lane == 1, sq, 0.0))
    traces[...] = jnp.broadcast_to(value.reshape(1, 1, 128), (WIDE, 1, 128))
    reorder = reorder_matrix()
    for j in range(3):
        tiles = [x[j, o] for o in range(ORB)]
        if masks[j] is not None:
            tiles = [t * masks[j].astype(BF16) for t in tiles]
        for r in range(ROWS):
            value = packed_row(tiles, r, True)
            if r == 0:
                a_first[j] = value
            elif r == ROWS - 1:
                a_last[j] = value
            else:
                a_mid[r - 1, j] = value
            if j == 1:
                turned = jnp.dot(reorder, value, preferred_element_type=F32).astype(BF16)
                put_panel(gb, ROWS, r, turned)


def deal_kernel(wanted, quad):
    step = 128
    for k in range(0, 1024, step):
        lanes = lax.broadcasted_iota(jnp.int32, (step, 1024), 1)
        quad[k : k + step, :] = jnp.where(lanes == wanted[k : k + step, :], 1.0, 0.0).astype(BF16)


def nt(a, b):
    return lax.dot_general(a, b, (((1,), (1,)), ((), ())), preferred_element_type=F32)


def tn(a, b):
    return lax.dot_general(a, b, (((0,), (0,)), ((), ())), preferred_element_type=F32)


def twice_weight(sums, rows_total):
    total = sums[0][...] + sums[1][...] + sums[2][...] + sums[3][...]
    tx = total[:, 0:1]
    sq = total[:, 1:2]
    return 2.0 * jax.nn.sigmoid(4.0 * (tx - sq) / (rows_total * BLOCK) + 5.0)


def assemble(full, base, count, sources):
    narrow = lax.axis_index("narrow")
    if len(sources) == NARROW:
        places = tuple((shift, 0, ORB) for shift in range(NARROW))
    else:
        places = ((0, 0, ORB), (1, 0, ORB), (2, 0, 5), (2, 5, 4), (3, 0, ORB))
    for (shift, o, depth), src in zip(places, sources):
        owner = lax.rem(narrow + shift, NARROW)
        for p in range(count):
            value = src[:, p * MAIN : (p + 1) * MAIN]
            full[base + p, o : o + depth, pl.ds(owner, 1), :, :MAIN] = value.reshape(
                depth, 1, 16, MAIN
            )
            tail = count * MAIN + p * ATOMS
            value = src[:, tail : tail + ATOMS]
            full[base + p, o : o + depth, pl.ds(owner, 1), :, MAIN:BLOCK] = value.reshape(
                depth, 1, 16, ATOMS
            )


def put_fresh(rows, value, r, s, slabs):
    for g in range(2):
        piece = value[:, g * 256 : (g + 1) * 256].astype(BF16)
        lanes = slice(r * 256, (r + 1) * 256)
        begin = (g * slabs + s) * 128
        rows[begin : begin + 128, lanes] = piece[:128]
        begin = slabs * 256 + (g * slabs + s) * 16
        rows[begin : begin + 16, lanes] = piece[128:]


def outer_kernel(
    rows_total, sum0, sum1, sum2, sum3, ga0, ga1, ga2, ga3, ga4,
    a_prev, a_first, a_mid, a_last, a_next, quad,
    out, left_over, full, rows, held, sems,
):
    gas = (ga0, ga1, ga2, ga3, ga4)
    twice = twice_weight((sum0, sum1, sum2, sum3), rows_total)
    assemble(full, 0, ROWS + 1, gas)
    lefts = [a_prev, a_first, a_mid.at[0], a_mid.at[1], a_last, a_next]
    left_over[...] = jnp.zeros_like(left_over)
    for r in range(ROWS):
        for s in range(2):
            if s == 0:
                b = full[r].reshape(BLOCK, LANES)
                prod = jnp.dot(lefts[r][0][:, :BLOCK], b, preferred_element_type=F32)
            elif r < ROWS - 1:
                b = full[r + 1].reshape(BLOCK, LANES)[:, :BLOCK]
                prod = nt(lefts[r + 2][2][:, :BLOCK], b)
            else:
                b = full[ROWS].reshape(BLOCK, LANES)
                prod = jnp.dot(lefts[r + 2][2][:, :BLOCK], b, preferred_element_type=F32)
            value = prod + twice * (0.0 - prod)
            put_fresh(rows, value, r, s, 2)
            tail = value[:, MAIN:BLOCK].astype(BF16)
            for half in range(2):
                lane = r * 256 + (2 * s + half) * ATOMS
                rows[576:640, lane : lane + ATOMS] = tail[half * 64 : half * 64 + 64]
            lane = r * 256 + s * ATOMS
            left_over[:, lane : lane + ATOMS] = tail[128:]
    copies = []
    for k in range(0, 1024, 256):
        held[k : k + 256, :] = nt(quad[k : k + 256, :], rows[...]).astype(BF16)
        copies.append(
            pltpu.make_async_copy(
                held.at[k : k + 256], out.at[k : k + 256], sems.at[len(copies)]
            )
        )
        copies[-1].start()
    for copy in copies:
        copy.wait()


def inner_kernel(
    rows_total, sum0, sum1, sum2, sum3, ga0, ga1, ga2, ga3, ga4, gb0, gb1, gb2, gb3,
    a_prev, a_first, a_mid, a_last, a_next, quad, left_over,
    out, full, acc, rows,
):
    gas = (ga0, ga1, ga2, ga3, ga4)
    gbs = (gb0, gb1, gb2, gb3)
    twice = twice_weight((sum0, sum1, sum2, sum3), rows_total)
    assemble(full, 0, ROWS + 1, gas)
    assemble(full, ROWS + 1, ROWS, gbs)
    lefts = [a_prev, a_first, a_mid.at[0], a_mid.at[1], a_last, a_next]

    def left(r, low, high):
        return jnp.concatenate([lefts[r + 1][j][:, :BLOCK] for j in range(low, high)], axis=0)

    rows[960:976, :] = jnp.zeros((16, 1024), BF16)
    rows[976:992, :] = left_over[...]
    rows[992:, :] = jnp.zeros((32, 1024), BF16)
    for r in range(ROWS):
        value = jnp.dot(
            left(r, 0, 3), full[ROWS + 1 + r].reshape(BLOCK, LANES), preferred_element_type=F32
        )
        for s in range(3):
            acc[s] = value[s * PANEL : (s + 1) * PANEL]
        value = jnp.dot(
            left(r - 1, 1, 3), full[r].reshape(BLOCK, LANES), preferred_element_type=F32
        )
        for s in range(2):
            acc[s] += value[s * PANEL : (s + 1) * PANEL]
        if r < ROWS - 1:
            value = nt(left(r + 1, 0, 2), full[r + 1].reshape(BLOCK, LANES)[:, :BLOCK])
        else:
            value = jnp.dot(
                left(r + 1, 0, 2), full[ROWS].reshape(BLOCK, LANES), preferred_element_type=F32
            )[:, :BLOCK]
        for s in range(2):
            acc[s + 1, :, :BLOCK] += value[s * PANEL : (s + 1) * PANEL]
        for s in range(3):
            prod = acc[s]
            value = prod + twice * (lefts[r + 1][s].astype(F32) - prod)
            put_fresh(rows, value, r, s, 3)
            tail = value[:, MAIN:BLOCK].astype(BF16)
            for q, (low, high) in enumerate(INNER_QUARTERS):
                begin, end = max(low, s * PANEL), min(high, (s + 1) * PANEL)
                if begin < end:
                    lane = r * 256 + q * ATOMS
                    rows[864 + begin - low : 864 + end - low, lane : lane + ATOMS] = tail[
                        begin - s * PANEL : end - s * PANEL
                    ]
    for k in range(0, 1024, 256):
        out[k : k + 256, :] = nt(quad[k : k + 256, :], rows[...]).astype(BF16)


def spread_matrix():
    i = lax.broadcasted_iota(jnp.int32, (512, 512), 0)
    lane = lax.broadcasted_iota(jnp.int32, (512, 512), 1)
    wanted = ((i // 4) % 4) * 128 + (i // 16) * 4 + i % 4
    return jnp.where(lane == wanted, 1.0, 0.0).astype(BF16)


def spread_out(z, lanes, spread):
    for half in range(2):
        value = tn(z[half * 512 : (half + 1) * 512, lanes], spread[...]).astype(BF16)
        for q in range(4):
            yield q, slice(half * 128, (half + 1) * 128), value[:, q * 128 : (q + 1) * 128]


def unpack_outer_kernel(z, out, spread, held, sems):
    spread[...] = spread_matrix()
    copies = []

    def send(o, s, high):
        row = s * 4 * PANEL
        copies.append(
            pltpu.make_async_copy(
                held.at[o, s, :high], out.at[o, row : row + high], sems.at[len(copies)]
            )
        )
        copies[-1].start()

    for q, lanes, value in spread_out(z, slice(512, 640), spread):
        held[8, q // 2, (q % 2) * 64 : (q % 2) * 64 + 64, lanes] = value[64:]
        for g in range(2):
            for s in range(2):
                begin = g * 32 + s * 16
                held[4 * g + q, s, 128:, lanes] = value[begin : begin + 16]
    for s in range(2):
        send(8, s, 128)
    for g in range(2):
        for q, lanes, value in spread_out(z, slice(g * 256, (g + 1) * 256), spread):
            for s in range(2):
                held[4 * g + q, s, :128, lanes] = value[s * 128 : (s + 1) * 128]
        for q in range(4):
            for s in range(2):
                send(4 * g + q, s, PANEL)
    for copy in copies:
        copy.wait()


def unpack_inner_kernel(z, begun, out, spread, held, edge, sems):
    del begun
    spread[...] = spread_matrix()
    copies = []

    def send(src, dst):
        copies.append(pltpu.make_async_copy(src, dst, sems.at[len(copies)]))
        copies[-1].start()

    for q, lanes, value in spread_out(z, slice(768, 1024), spread):
        low, high = INNER_QUARTERS[q]
        held[8, low:high, lanes] = value[96 : 96 + high - low]
        if q < 2:
            edge[q, :, lanes] = value[208:224]
        for g in range(2):
            for s in range(3):
                begin = g * 48 + s * 16
                held[4 * g + q, s * PANEL + 128 : (s + 1) * PANEL, lanes] = value[
                    begin : begin + 16
                ]
    send(held.at[8], out.at[8, PANEL : 4 * PANEL])
    for s in range(2):
        row = s * 4 * PANEL + 128
        send(edge.at[s], out.at[8, row : row + 16])
    for g in range(2):
        for q, lanes, value in spread_out(z, slice(g * 384, (g + 1) * 384), spread):
            for s in range(3):
                held[4 * g + q, s * PANEL : s * PANEL + 128, lanes] = value[
                    s * 128 : (s + 1) * 128
                ]
        for q in range(4):
            send(held.at[4 * g + q], out.at[4 * g + q, PANEL : 4 * PANEL])
    for copy in copies:
        copy.wait()


def shift_perm(count, step):
    return [(i, (i - step) % count) for i in range(count)]


def neighbours(own):
    after = lax.ppermute(own, "narrow", shift_perm(NARROW, 1))
    before = lax.ppermute(own, "narrow", shift_perm(NARROW, -1))
    return after, before


def opposite(after, before):
    split = 80
    top, bottom = lax.optimization_barrier((after[:split], before[split:]))
    top = lax.ppermute(top, "narrow", shift_perm(NARROW, 1))
    bottom = lax.ppermute(bottom, "narrow", shift_perm(NARROW, -1))
    return top, bottom


def direct_gather(own):
    return [own] + [lax.ppermute(own, "narrow", shift_perm(NARROW, step)) for step in (1, 2, 3)]


def exchange(packed, chunk):
    parts = packed.reshape(WIDE, 16, chunk)
    got = lax.all_to_all(parts, "wide", split_axis=0, concat_axis=0, tiled=True)
    return got.reshape(1024, chunk)


def shards(xblk, link, order):
    rows_total = link.shape[0]
    x = jnp.transpose(xblk, (0, 2, 1, 3))
    slab = (1, ORB, PANEL, ROWS * ATOMS)
    ga = pl.pallas_call(
        prep_outer_kernel,
        out_shape=sds((PANEL, 2944), BF16),
        grid=(1,),
        in_specs=[
            SM,
            pl.BlockSpec(slab, lambda i: (0, 0, 0, 0)),
            pl.BlockSpec(slab, lambda i: (2, 0, 0, 0)),
        ],
        out_specs=pl.BlockSpec((PANEL, 2944), lambda i: (0, 0)),
        compiler_params=params(48),
        name="prep_outer",
    )(link, x, x)
    after, before = neighbours(ga)
    gb, a_first, a_mid, a_last, traces = pl.pallas_call(
        prep_inner_kernel,
        out_shape=[
            sds((PANEL, 2304), BF16),
            sds((3, PANEL, LANES), BF16),
            sds((2, 3, PANEL, LANES), BF16),
            sds((3, PANEL, LANES), BF16),
            sds((WIDE, 1, 128), F32),
        ],
        in_specs=[SM, VM, ANY],
        out_specs=[VM] * 5,
        compiler_params=params(52),
        name="prep_inner",
    )(link, x, ga)
    a_prev = lax.ppermute(a_last, "wide", shift_perm(WIDE, -1))
    a_next = lax.ppermute(a_first, "wide", shift_perm(WIDE, 1))
    line = lax.all_to_all(traces, "wide", split_axis=0, concat_axis=0, tiled=True)
    line = jnp.sum(line, axis=0)
    sums = direct_gather(line)
    after, before, a_prev, a_next = lax.optimization_barrier((after, before, a_prev, a_next))
    gas = (ga, after, *opposite(after, before), before)
    wanted = jnp.broadcast_to(order.reshape(64, 1, 4), (64, 4, 4))
    quarter = jnp.arange(4, dtype=jnp.int32).reshape(1, 4, 1)
    wanted = ((wanted // ATOMS) * 256 + quarter * ATOMS + wanted % ATOMS).reshape(1024, 1)
    quad = pl.pallas_call(
        deal_kernel,
        out_shape=sds((1024, 1024), BF16),
        in_specs=[VM],
        out_specs=VM,
        compiler_params=params(8),
        name="deal",
    )(wanted)
    gb, quad, a_prev, a_next = lax.optimization_barrier((gb, quad, a_prev, a_next))
    gbs = direct_gather(gb)
    lefts = (a_prev, a_first, a_mid, a_last, a_next)
    packed_outer, left_over = pl.pallas_call(
        lambda *refs: outer_kernel(rows_total, *refs),
        out_shape=[sds((1024, OUTER_CHUNK), BF16), sds((16, 1024), BF16)],
        in_specs=[VM] * 15,
        out_specs=[HBM, VM],
        scratch_shapes=[
            pltpu.VMEM((ROWS + 1, ORB, NARROW, 16, LANES), BF16),
            pltpu.VMEM((OUTER_CHUNK, 1024), BF16),
            pltpu.VMEM((1024, OUTER_CHUNK), BF16),
            pltpu.SemaphoreType.DMA((4,)),
        ],
        compiler_params=params(24),
        cost_estimate=pl.CostEstimate(
            flops=OUTER_FLOPS, bytes_accessed=8 << 20, transcendentals=0
        ),
        name="outer",
    )(*sums, *gas, *lefts, quad)
    got_outer = exchange(packed_outer, OUTER_CHUNK)
    packed_inner = pl.pallas_call(
        lambda *refs: inner_kernel(rows_total, *refs),
        out_shape=sds((1024, INNER_CHUNK), BF16),
        in_specs=[VM] * 20,
        out_specs=VM,
        scratch_shapes=[
            pltpu.VMEM((2 * ROWS + 1, ORB, NARROW, 16, LANES), BF16),
            pltpu.VMEM((3, PANEL, LANES), F32),
            pltpu.VMEM((INNER_CHUNK, 1024), BF16),
        ],
        compiler_params=params(54),
        cost_estimate=pl.CostEstimate(
            flops=INNER_FLOPS, bytes_accessed=12 << 20, transcendentals=0
        ),
        name="inner",
    )(*sums, *gas, *gbs, *lefts, quad, left_over)
    packed_inner, got_outer = lax.optimization_barrier((packed_inner, got_outer))
    got_inner = exchange(packed_inner, INNER_CHUNK)
    out = pl.pallas_call(
        unpack_outer_kernel,
        out_shape=sds((ORB, 5 * PANEL, 256), BF16),
        in_specs=[VM],
        out_specs=ANY,
        scratch_shapes=[
            pltpu.VMEM((512, 512), BF16),
            pltpu.VMEM((ORB, 2, PANEL, 256), BF16),
            pltpu.SemaphoreType.DMA((18,)),
        ],
        compiler_params=params(14),
        name="unpack_outer",
    )(got_outer)
    out = pl.pallas_call(
        unpack_inner_kernel,
        out_shape=sds((ORB, 5 * PANEL, 256), BF16),
        in_specs=[VM, ANY],
        out_specs=ANY,
        scratch_shapes=[
            pltpu.VMEM((512, 512), BF16),
            pltpu.VMEM((ORB, 3 * PANEL, 256), BF16),
            pltpu.VMEM((2, 16, 256), BF16),
            pltpu.SemaphoreType.DMA((11,)),
        ],
        input_output_aliases={1: 0},
        compiler_params=params(16),
        name="unpack_inner",
    )(got_inner, out)
    return out.reshape(ORB, 5, PANEL, 256)


def solution(mesh):
    return jax.shard_map(
        shards,
        mesh=mesh,
        in_specs=(P(None, "narrow", None, "wide"), P(), P("wide")),
        out_specs=P(None, None, "narrow", "wide"),
        check_vma=False,
    )
```

```python
import jax
import jax.numpy as jnp
from jax import lax
from jax.experimental import pallas as pl
from jax.experimental.pallas import tpu as pltpu
from jax.sharding import PartitionSpec as P

ORB = 9
ATOMS = 64
BLOCK = 576
PANEL = 144
LANES = 640
ROWS = 4
NARROW = 4
WIDE = 64
MAIN = 512
OUTER_CHUNK = 640
INNER_CHUNK = 1024
INNER_QUARTERS = ((0, 112), (112, 224), (224, 336), (336, 432))
F32 = jnp.float32
BF16 = jnp.bfloat16
OUTER_FLOPS = 30 * 10**9
INNER_FLOPS = 70 * 10**9

VM = pl.BlockSpec(memory_space=pltpu.VMEM)
SM = pl.BlockSpec(memory_space=pltpu.SMEM)
ANY = pl.BlockSpec(memory_space=pl.ANY)
HBM = pl.BlockSpec(memory_space=pltpu.HBM)
sds = jax.ShapeDtypeStruct


def params(mib):
    return pltpu.CompilerParams(vmem_limit_bytes=mib << 20)


def lane_mask(link, first, shift):
    lanes = lax.broadcasted_iota(jnp.int32, (1, ROWS * ATOMS), 1) // ATOMS
    total = link.shape[0]
    mask = jnp.zeros((1, ROWS * ATOMS), F32)
    for r in range(ROWS):
        value = link[lax.rem(first + (r + shift + total), total)].astype(F32)
        mask = jnp.where(lanes == r, value, mask)
    return mask


def reorder_matrix():
    i = lax.broadcasted_iota(jnp.int32, (PANEL, PANEL), 0)
    c = lax.broadcasted_iota(jnp.int32, (PANEL, PANEL), 1)
    return jnp.where(c == (i % 16) * ORB + i // 16, 1.0, 0.0).astype(BF16)


def packed_row(tiles, r, pad):
    parts = [t[:, r * ATOMS : (r + 1) * ATOMS] for t in tiles]
    if pad:
        parts.append(jnp.zeros((PANEL, ATOMS), BF16))
    return jnp.concatenate(parts, axis=1)


def put_panel(out, count, p, value):
    out[:, p * MAIN : (p + 1) * MAIN] = value[:, :MAIN]
    tail = count * MAIN + p * ATOMS
    out[:, tail : tail + ATOMS] = value[:, MAIN:BLOCK]


def prep_outer_kernel(link, low, high, ga):
    first = lax.axis_index("wide") * ROWS
    before = lane_mask(link, first, -1).astype(BF16)
    after = lane_mask(link, first, 0).astype(BF16)
    reorder = reorder_matrix()
    tiles = [low[0, o] * before for o in range(ORB)]
    for p in range(ROWS + 1):
        if p == ROWS:
            tiles = [high[0, o] * after for o in range(ORB)]
        value = packed_row(tiles, min(p, ROWS - 1), False)
        turned = jnp.dot(reorder, value, preferred_element_type=F32).astype(BF16)
        put_panel(ga, ROWS + 1, p, turned)
    ga[:, (ROWS + 1) * BLOCK :] = jnp.zeros((PANEL, ATOMS), BF16)


def prep_inner_kernel(link, x, ga, gb, a_first, a_mid, a_last, traces):
    del ga
    first = lax.axis_index("wide") * ROWS
    masks = (lane_mask(link, first, -1), None, lane_mask(link, first, 0))
    squares = jnp.zeros((PANEL, ROWS * ATOMS), F32)
    for j in range(3):
        total = jnp.zeros((PANEL, ROWS * ATOMS), F32)
        for o in range(ORB):
            t = x[j, o].astype(F32)
            total = total + t * t
        if masks[j] is not None:
            total = total * masks[j]
        squares = squares + total
    narrow = lax.axis_index("narrow")
    rows = lax.broadcasted_iota(jnp.int32, (PANEL, ROWS * ATOMS), 0) + narrow * PANEL
    lanes = lax.broadcasted_iota(jnp.int32, (PANEL, ROWS * ATOMS), 1) % ATOMS
    diagonal = jnp.zeros((PANEL, ROWS * ATOMS), F32)
    for o in range(ORB):
        diagonal = diagonal + jnp.where(rows == lanes * ORB + o, x[1, o].astype(F32), 0.0)
    sq = jnp.sum(squares, axis=0, keepdims=True)
    tx = jnp.sum(diagonal, axis=0, keepdims=True)
    sq = jnp.sum(sq, axis=1, keepdims=True)
    tx = jnp.sum(tx, axis=1, keepdims=True)
    lane = lax.broadcasted_iota(jnp.int32, (1, 128), 1)
    value = jnp.where(lane == 0, tx, jnp.where(lane == 1, sq, 0.0))
    traces[...] = jnp.broadcast_to(value.reshape(1, 1, 128), (WIDE, 1, 128))
    reorder = reorder_matrix()
    for j in range(3):
        tiles = [x[j, o] for o in range(ORB)]
        if masks[j] is not None:
            tiles = [t * masks[j].astype(BF16) for t in tiles]
        for r in range(ROWS):
            value = packed_row(tiles, r, True)
            if r == 0:
                a_first[j] = value
            elif r == ROWS - 1:
                a_last[j] = value
            else:
                a_mid[r - 1, j] = value
            if j == 1:
                turned = jnp.dot(reorder, value, preferred_element_type=F32).astype(BF16)
                put_panel(gb, ROWS, r, turned)


def deal_kernel(wanted, quad):
    step = 128
    for k in range(0, 1024, step):
        lanes = lax.broadcasted_iota(jnp.int32, (step, 1024), 1)
        quad[k : k + step, :] = jnp.where(lanes == wanted[k : k + step, :], 1.0, 0.0).astype(BF16)


def nt(a, b):
    return lax.dot_general(a, b, (((1,), (1,)), ((), ())), preferred_element_type=F32)


def tn(a, b):
    return lax.dot_general(a, b, (((0,), (0,)), ((), ())), preferred_element_type=F32)


def twice_weight(sums, rows_total):
    total = sums[0][...] + sums[1][...] + sums[2][...] + sums[3][...]
    tx = total[:, 0:1]
    sq = total[:, 1:2]
    return 2.0 * jax.nn.sigmoid(4.0 * (tx - sq) / (rows_total * BLOCK) + 5.0)


def assemble(full, base, count, sources):
    narrow = lax.axis_index("narrow")
    if len(sources) == NARROW:
        places = tuple((shift, 0, ORB) for shift in range(NARROW))
    else:
        places = ((0, 0, ORB), (1, 0, ORB), (2, 0, 5), (2, 5, 4), (3, 0, ORB))
    for (shift, o, depth), src in zip(places, sources):
        owner = lax.rem(narrow + shift, NARROW)
        for p in range(count):
            value = src[:, p * MAIN : (p + 1) * MAIN]
            full[base + p, o : o + depth, pl.ds(owner, 1), :, :MAIN] = value.reshape(
                depth, 1, 16, MAIN
            )
            tail = count * MAIN + p * ATOMS
            value = src[:, tail : tail + ATOMS]
            full[base + p, o : o + depth, pl.ds(owner, 1), :, MAIN:BLOCK] = value.reshape(
                depth, 1, 16, ATOMS
            )


def put_fresh(rows, value, r, s, slabs):
    for g in range(2):
        piece = value[:, g * 256 : (g + 1) * 256].astype(BF16)
        lanes = slice(r * 256, (r + 1) * 256)
        begin = (g * slabs + s) * 128
        rows[begin : begin + 128, lanes] = piece[:128]
        begin = slabs * 256 + (g * slabs + s) * 16
        rows[begin : begin + 16, lanes] = piece[128:]


def outer_kernel(
    rows_total, sum0, sum1, sum2, sum3, ga0, ga1, ga2, ga3, ga4,
    a_prev, a_first, a_mid, a_last, a_next, quad,
    out, left_over, full, rows, held, sems,
):
    gas = (ga0, ga1, ga2, ga3, ga4)
    twice = twice_weight((sum0, sum1, sum2, sum3), rows_total)
    assemble(full, 0, ROWS + 1, gas)
    lefts = [a_prev, a_first, a_mid.at[0], a_mid.at[1], a_last, a_next]
    left_over[...] = jnp.zeros_like(left_over)
    for r in range(ROWS):
        for s in range(2):
            if s == 0:
                b = full[r].reshape(BLOCK, LANES)
                prod = jnp.dot(lefts[r][0][:, :BLOCK], b, preferred_element_type=F32)
            elif r < ROWS - 1:
                b = full[r + 1].reshape(BLOCK, LANES)[:, :BLOCK]
                prod = nt(lefts[r + 2][2][:, :BLOCK], b)
            else:
                b = full[ROWS].reshape(BLOCK, LANES)
                prod = jnp.dot(lefts[r + 2][2][:, :BLOCK], b, preferred_element_type=F32)
            value = prod + twice * (0.0 - prod)
            put_fresh(rows, value, r, s, 2)
            tail = value[:, MAIN:BLOCK].astype(BF16)
            for half in range(2):
                lane = r * 256 + (2 * s + half) * ATOMS
                rows[576:640, lane : lane + ATOMS] = tail[half * 64 : half * 64 + 64]
            lane = r * 256 + s * ATOMS
            left_over[:, lane : lane + ATOMS] = tail[128:]
    copies = []
    for k in range(0, 1024, 256):
        held[k : k + 256, :] = nt(quad[k : k + 256, :], rows[...]).astype(BF16)
        copies.append(
            pltpu.make_async_copy(
                held.at[k : k + 256], out.at[k : k + 256], sems.at[len(copies)]
            )
        )
        copies[-1].start()
    for copy in copies:
        copy.wait()


def inner_kernel(
    rows_total, sum0, sum1, sum2, sum3, ga0, ga1, ga2, ga3, ga4, gb0, gb1, gb2, gb3,
    a_prev, a_first, a_mid, a_last, a_next, quad, left_over,
    out, full, acc, rows,
):
    gas = (ga0, ga1, ga2, ga3, ga4)
    gbs = (gb0, gb1, gb2, gb3)
    twice = twice_weight((sum0, sum1, sum2, sum3), rows_total)
    assemble(full, 0, ROWS + 1, gas)
    assemble(full, ROWS + 1, ROWS, gbs)
    lefts = [a_prev, a_first, a_mid.at[0], a_mid.at[1], a_last, a_next]

    def left(r, low, high):
        return jnp.concatenate([lefts[r + 1][j][:, :BLOCK] for j in range(low, high)], axis=0)

    rows[960:976, :] = jnp.zeros((16, 1024), BF16)
    rows[976:992, :] = left_over[...]
    rows[992:, :] = jnp.zeros((32, 1024), BF16)
    for r in range(ROWS):
        value = jnp.dot(
            left(r, 0, 3), full[ROWS + 1 + r].reshape(BLOCK, LANES), preferred_element_type=F32
        )
        for s in range(3):
            acc[s] = value[s * PANEL : (s + 1) * PANEL]
        value = jnp.dot(
            left(r - 1, 1, 3), full[r].reshape(BLOCK, LANES), preferred_element_type=F32
        )
        for s in range(2):
            acc[s] += value[s * PANEL : (s + 1) * PANEL]
        if r < ROWS - 1:
            value = nt(left(r + 1, 0, 2), full[r + 1].reshape(BLOCK, LANES)[:, :BLOCK])
        else:
            value = jnp.dot(
                left(r + 1, 0, 2), full[ROWS].reshape(BLOCK, LANES), preferred_element_type=F32
            )[:, :BLOCK]
        for s in range(2):
            acc[s + 1, :, :BLOCK] += value[s * PANEL : (s + 1) * PANEL]
        for s in range(3):
            prod = acc[s]
            value = prod + twice * (lefts[r + 1][s].astype(F32) - prod)
            put_fresh(rows, value, r, s, 3)
            tail = value[:, MAIN:BLOCK].astype(BF16)
            for q, (low, high) in enumerate(INNER_QUARTERS):
                begin, end = max(low, s * PANEL), min(high, (s + 1) * PANEL)
                if begin < end:
                    lane = r * 256 + q * ATOMS
                    rows[864 + begin - low : 864 + end - low, lane : lane + ATOMS] = tail[
                        begin - s * PANEL : end - s * PANEL
                    ]
    for k in range(0, 1024, 256):
        out[k : k + 256, :] = nt(quad[k : k + 256, :], rows[...]).astype(BF16)


def spread_matrix():
    i = lax.broadcasted_iota(jnp.int32, (512, 512), 0)
    lane = lax.broadcasted_iota(jnp.int32, (512, 512), 1)
    wanted = ((i // 4) % 4) * 128 + (i // 16) * 4 + i % 4
    return jnp.where(lane == wanted, 1.0, 0.0).astype(BF16)


def spread_out(z, lanes, spread):
    for half in range(2):
        value = tn(z[half * 512 : (half + 1) * 512, lanes], spread[...]).astype(BF16)
        for q in range(4):
            yield q, slice(half * 128, (half + 1) * 128), value[:, q * 128 : (q + 1) * 128]


def unpack_outer_kernel(z, out, spread, held, sems):
    spread[...] = spread_matrix()
    copies = []

    def send(o, s, high):
        row = s * 4 * PANEL
        copies.append(
            pltpu.make_async_copy(
                held.at[o, s, :high], out.at[o, row : row + high], sems.at[len(copies)]
            )
        )
        copies[-1].start()

    for q, lanes, value in spread_out(z, slice(512, 640), spread):
        held[8, q // 2, (q % 2) * 64 : (q % 2) * 64 + 64, lanes] = value[64:]
        for g in range(2):
            for s in range(2):
                begin = g * 32 + s * 16
                held[4 * g + q, s, 128:, lanes] = value[begin : begin + 16]
    for s in range(2):
        send(8, s, 128)
    for g in range(2):
        for q, lanes, value in spread_out(z, slice(g * 256, (g + 1) * 256), spread):
            for s in range(2):
                held[4 * g + q, s, :128, lanes] = value[s * 128 : (s + 1) * 128]
        for q in range(4):
            for s in range(2):
                send(4 * g + q, s, PANEL)
    for copy in copies:
        copy.wait()


def unpack_inner_kernel(z, begun, out, spread, held, edge, sems):
    del begun
    spread[...] = spread_matrix()
    copies = []

    def send(src, dst):
        copies.append(pltpu.make_async_copy(src, dst, sems.at[len(copies)]))
        copies[-1].start()

    for q, lanes, value in spread_out(z, slice(768, 1024), spread):
        low, high = INNER_QUARTERS[q]
        held[8, low:high, lanes] = value[96 : 96 + high - low]
        if q < 2:
            edge[q, :, lanes] = value[208:224]
        for g in range(2):
            for s in range(3):
                begin = g * 48 + s * 16
                held[4 * g + q, s * PANEL + 128 : (s + 1) * PANEL, lanes] = value[
                    begin : begin + 16
                ]
    send(held.at[8], out.at[8, PANEL : 4 * PANEL])
    for s in range(2):
        row = s * 4 * PANEL + 128
        send(edge.at[s], out.at[8, row : row + 16])
    for g in range(2):
        for q, lanes, value in spread_out(z, slice(g * 384, (g + 1) * 384), spread):
            for s in range(3):
                held[4 * g + q, s * PANEL : s * PANEL + 128, lanes] = value[
                    s * 128 : (s + 1) * 128
                ]
        for q in range(4):
            send(held.at[4 * g + q], out.at[4 * g + q, PANEL : 4 * PANEL])
    for copy in copies:
        copy.wait()


def shift_perm(count, step):
    return [(i, (i - step) % count) for i in range(count)]


def neighbours(own):
    after = lax.ppermute(own, "narrow", shift_perm(NARROW, 1))
    before = lax.ppermute(own, "narrow", shift_perm(NARROW, -1))
    return after, before


def opposite(after, before):
    split = 80
    top, bottom = lax.optimization_barrier((after[:split], before[split:]))
    top = lax.ppermute(top, "narrow", shift_perm(NARROW, 1))
    bottom = lax.ppermute(bottom, "narrow", shift_perm(NARROW, -1))
    return top, bottom


def direct_gather(own):
    return [own] + [lax.ppermute(own, "narrow", shift_perm(NARROW, step)) for step in (1, 2, 3)]


def exchange(packed, chunk):
    parts = packed.reshape(WIDE, 16, chunk)
    got = lax.all_to_all(parts, "wide", split_axis=0, concat_axis=0, tiled=True)
    return got.reshape(1024, chunk)


def shards(xblk, link, order):
    rows_total = link.shape[0]
    x = jnp.transpose(xblk, (0, 2, 1, 3))
    slab = (1, ORB, PANEL, ROWS * ATOMS)
    ga = pl.pallas_call(
        prep_outer_kernel,
        out_shape=sds((PANEL, 2944), BF16),
        grid=(1,),
        in_specs=[
            SM,
            pl.BlockSpec(slab, lambda i: (0, 0, 0, 0)),
            pl.BlockSpec(slab, lambda i: (2, 0, 0, 0)),
        ],
        out_specs=pl.BlockSpec((PANEL, 2944), lambda i: (0, 0)),
        compiler_params=params(52),
        name="prep_outer",
    )(link, x, x)
    after, before = neighbours(ga)
    gb, a_first, a_mid, a_last, traces = pl.pallas_call(
        prep_inner_kernel,
        out_shape=[
            sds((PANEL, 2304), BF16),
            sds((3, PANEL, LANES), BF16),
            sds((2, 3, PANEL, LANES), BF16),
            sds((3, PANEL, LANES), BF16),
            sds((WIDE, 1, 128), F32),
        ],
        in_specs=[SM, VM, ANY],
        out_specs=[VM] * 5,
        compiler_params=params(52),
        name="prep_inner",
    )(link, x, ga)
    a_prev = lax.ppermute(a_last, "wide", shift_perm(WIDE, -1))
    a_next = lax.ppermute(a_first, "wide", shift_perm(WIDE, 1))
    line = lax.all_to_all(traces, "wide", split_axis=0, concat_axis=0, tiled=True)
    line = jnp.sum(line, axis=0)
    sums = direct_gather(line)
    after, before, a_prev, a_next = lax.optimization_barrier((after, before, a_prev, a_next))
    gas = (ga, after, *opposite(after, before), before)
    wanted = jnp.broadcast_to(order.reshape(64, 1, 4), (64, 4, 4))
    quarter = jnp.arange(4, dtype=jnp.int32).reshape(1, 4, 1)
    wanted = ((wanted // ATOMS) * 256 + quarter * ATOMS + wanted % ATOMS).reshape(1024, 1)
    quad = pl.pallas_call(
        deal_kernel,
        out_shape=sds((1024, 1024), BF16),
        in_specs=[VM],
        out_specs=VM,
        compiler_params=params(8),
        name="deal",
    )(wanted)
    gb, quad, a_prev, a_next = lax.optimization_barrier((gb, quad, a_prev, a_next))
    gbs = direct_gather(gb)
    lefts = (a_prev, a_first, a_mid, a_last, a_next)
    packed_outer, left_over = pl.pallas_call(
        lambda *refs: outer_kernel(rows_total, *refs),
        out_shape=[sds((1024, OUTER_CHUNK), BF16), sds((16, 1024), BF16)],
        in_specs=[VM] * 15,
        out_specs=[HBM, VM],
        scratch_shapes=[
            pltpu.VMEM((ROWS + 1, ORB, NARROW, 16, LANES), BF16),
            pltpu.VMEM((OUTER_CHUNK, 1024), BF16),
            pltpu.VMEM((1024, OUTER_CHUNK), BF16),
            pltpu.SemaphoreType.DMA((4,)),
        ],
        compiler_params=params(24),
        cost_estimate=pl.CostEstimate(
            flops=OUTER_FLOPS, bytes_accessed=8 << 20, transcendentals=0
        ),
        name="outer",
    )(*sums, *gas, *lefts, quad)
    got_outer = exchange(packed_outer, OUTER_CHUNK)
    packed_inner = pl.pallas_call(
        lambda *refs: inner_kernel(rows_total, *refs),
        out_shape=sds((1024, INNER_CHUNK), BF16),
        in_specs=[VM] * 20,
        out_specs=VM,
        scratch_shapes=[
            pltpu.VMEM((2 * ROWS + 1, ORB, NARROW, 16, LANES), BF16),
            pltpu.VMEM((3, PANEL, LANES), F32),
            pltpu.VMEM((INNER_CHUNK, 1024), BF16),
        ],
        compiler_params=params(54),
        cost_estimate=pl.CostEstimate(
            flops=INNER_FLOPS, bytes_accessed=12 << 20, transcendentals=0
        ),
        name="inner",
    )(*sums, *gas, *gbs, *lefts, quad, left_over)
    packed_inner, got_outer = lax.optimization_barrier((packed_inner, got_outer))
    got_inner = exchange(packed_inner, INNER_CHUNK)
    out = pl.pallas_call(
        unpack_outer_kernel,
        out_shape=sds((ORB, 5 * PANEL, 256), BF16),
        in_specs=[VM],
        out_specs=ANY,
        scratch_shapes=[
            pltpu.VMEM((512, 512), BF16),
            pltpu.VMEM((ORB, 2, PANEL, 256), BF16),
            pltpu.SemaphoreType.DMA((18,)),
        ],
        compiler_params=params(14),
        name="unpack_outer",
    )(got_outer)
    out = pl.pallas_call(
        unpack_inner_kernel,
        out_shape=sds((ORB, 5 * PANEL, 256), BF16),
        in_specs=[VM, ANY],
        out_specs=ANY,
        scratch_shapes=[
            pltpu.VMEM((512, 512), BF16),
            pltpu.VMEM((ORB, 3 * PANEL, 256), BF16),
            pltpu.VMEM((2, 16, 256), BF16),
            pltpu.SemaphoreType.DMA((11,)),
        ],
        input_output_aliases={1: 0},
        compiler_params=params(16),
        name="unpack_inner",
    )(got_inner, out)
    return out.reshape(ORB, 5, PANEL, 256)


def solution(mesh):
    return jax.shard_map(
        shards,
        mesh=mesh,
        in_specs=(P(None, "narrow", None, "wide"), P(), P("wide")),
        out_specs=P(None, None, "narrow", "wide"),
        check_vma=False,
    )
```
